512 devices in a mesh: dp: 64 (over y_hi, z, core), mp: 8 (over y_lo, x).
Axes of the slice: x: 4, y: 4 (y_hi: 2, y_lo: 2; y = y_hi * 2 + y_lo), z: 16, core: 2. Of those that a mesh axis runs over, the one named last changes fastest.
Arguments:
- queries: bfloat16 [2048, 4096], P('dp', 'mp'), may hold values from -16 to 16, as said below
- passages: bfloat16 [2048, 4096], P('dp', 'mp'), may hold values from -6 to 6, as said below
- negatives: bfloat16 [14336, 4096], P('dp', 'mp'), may hold values from -8 to 8
- hard_owner: int32 [2048, 7], P('dp'), may hold values from 0 to 63, all different within a row; in each aligned block of 32 rows (0 to 31, 32 to 63, ...) at most 7 rows name the same one
- hard_row: int32 [2048, 7], P('dp'), may hold values from 0 to 223
Outputs:
- query_grad: bfloat16 [2048, 4096], P('dp', 'mp')
- passage_grad: bfloat16 [2048, 4096], P('dp', 'mp')
- negative_grad: bfloat16 [14336, 4096], P('dp', 'mp')
The draws below stay inside these ranges and needn't reach their ends.
Inputs may be any that keep to these rules, and one draw needn't show every extreme that they name: In some draws a few queries are close to a multiple (up to 3) of some passage's direction, so that some in-batch scores reach several hundred. In some draws a few passages nearly repeat other passages. `hard_owner`: each query names 7 different owners; among the queries of one index of dp at most 7 references go to one owner, and in every draw some owner receives exactly 7 from some index. `hard_row`: rows may repeat across queries.
All inputs are finite; a program needn't handle non-finite values.
Results may differ from the reference program's by a relative error of at most 0.013.
Values may be sent and summed in bfloat16 or wider, within the bound.
No kernel may reach another device: no remote copies, remote signals or barrier semaphores. Data moves between devices by JAX's collectives and lax.ppermute only.
A program may use at most 64 MiB of HBM per device.

```python
import math
import jax
import jax.numpy as jnp
import numpy as np
from jax import lax

D = 4096
NEG = 7
Q_DEV = 32
NQ = 2048
NEG_DEV = 224
NN = 14336
CAP = 7
N_DP = 64


def shared_rows(key):
    key = jax.random.fold_in(key, 101)
    key_base = jax.random.fold_in(key, 0)
    base_rows = jax.random.truncated_normal(key_base, -4.0, 4.0, (NQ, D), jnp.float32)
    return base_rows


def draw_passages(key, part):
    base_rows = shared_rows(key)
    return base_rows.astype(jnp.bfloat16)


def draw_queries(key, part):
    key = jax.random.fold_in(key, 13)
    values = jax.random.truncated_normal(key, -4.0, 4.0, (NQ, D), jnp.float32)
    return values.astype(jnp.bfloat16)


def plant(drawn, stream_key, low, high):
    dims = drawn.shape
    spot = [jax.random.randint(jax.random.fold_in(stream_key, axis), (), 0, dims[axis]) for axis in range(len(dims))]
    drawn = drawn.at[tuple(spot)].set(low)
    longest = dims.index(max(dims))
    spot[longest] = (spot[longest] + 1) % dims[longest]
    return drawn.at[tuple(spot)].set(high)


def block_levels(stream_key, shape, shards, low, largest):
    level, own = 1.0, jax.random.fold_in(stream_key, 6)
    for axis_at, blocks in shards:
        draws = jnp.exp(jax.random.uniform(jax.random.fold_in(own, axis_at), (blocks,), jnp.float32, low / len(shards), largest / len(shards)))
        level = level * jnp.repeat(draws, shape[axis_at] // blocks).reshape([-1 if axis == axis_at else 1 for axis in range(len(shape))])
    return level


def assign_block(own_key, own, number, rows, count, top, bound, lean):
    order = jax.random.permutation(own_key, count)
    crowded, common = load_shares(count, rows * top, bound, lean, True), load_shares(count, rows * top, bound, lean, False)
    places = jnp.arange(count)

    def named(lengths, offset_by):
        used = int((lengths > 0).sum())
        fixed = max(1, used // 4)
        shifted = fixed + (places - fixed + offset_by * (used - fixed)) % max(1, count - fixed)
        return jnp.zeros((count,), jnp.int32).at[order[jnp.where(places < fixed, places, shifted)]].set(jnp.asarray(lengths, jnp.int32))

    lengths = jnp.where(number % 4 == 0, named(crowded, number // 4), named(common, number - number // 4 - 1))
    mixed = jax.random.permutation(jax.random.fold_in(own, 3), count)
    source_of, sink = mixed[0:count // 2 * 2:2], mixed[1:count // 2 * 2:2]
    margin = jnp.minimum(lengths[source_of] - 1, bound - lengths[sink]) // 2
    margin = jnp.where((source_of == order[0]) | (sink == order[0]) | (lengths[sink] == 0), 0, jnp.maximum(margin, 0))
    shifted = jax.random.randint(jax.random.fold_in(own, 4), (count // 2,), 0, 1 << 20) % (margin + 1)
    lengths = lengths.at[source_of].add(-shifted).at[sink].add(shifted)
    labels = jnp.searchsorted(jnp.cumsum(lengths), jnp.arange(rows * top), side="right").astype(jnp.int32)
    listing = labels.reshape(top, rows).T
    listing = listing[jax.random.permutation(jax.random.fold_in(own, 1), rows)]
    offset_by = jax.random.randint(jax.random.fold_in(own, 2), (rows, 1), 0, top)
    return jnp.take_along_axis(listing, (jnp.arange(top)[None, :] + offset_by) % top, axis=1)


def load_shares(count, total, bound, lean, full):
    loads = [(1 << 20) // math.isqrt(standing ** lean) + 1 for standing in range(1, count + 1)]
    largest = bound if full else min(bound, max(-(-total // count), total * loads[0] // sum(loads)))
    least = 1 if total - largest >= count - 1 else 0
    counts, surplus = [largest] + [least] * (count - 1), total - largest - least * (count - 1)
    while surplus > 0:
        candidates = [i for i in range(1, count) if counts[i] < largest] or [i for i in range(1, count) if counts[i] < bound]
        mass, budget = sum([loads[i] for i in candidates]), surplus
        for i in candidates:
            more = min(bound - counts[i], max(1, budget * loads[i] // mass), surplus)
            counts[i] = counts[i] + more
            surplus = surplus - more
    return np.array(counts)


def bell_draw(key, dims, scale, limit, cuts=(), kind=jnp.bfloat16):
    entries = scale * jax.random.normal(key, dims, jnp.float32)
    if cuts:
        entries = entries * block_levels(key, dims, cuts, -0.22, 0.18)
    return jnp.clip(entries, -limit, limit).astype(kind)


def setup_inputs(seed: int = 0) -> dict:
    keys = jax.random.split(jax.random.key(seed), 6)
    queries = draw_queries(jax.random.fold_in(keys[5], 71), 0)
    passages = draw_passages(jax.random.fold_in(keys[5], 71), 0)
    negatives = bell_draw(keys[2], (NN, D), 2.0, 8.0, ((0, 64), (1, 8)))
    hard_owner_keys = jax.random.split(jax.random.fold_in(keys[3], 1), NQ // Q_DEV)
    hard_owner_turns = jax.random.permutation(jax.random.fold_in(keys[3], 3), NQ // Q_DEV)
    hard_owner = jax.vmap(lambda own, number: assign_block(jax.random.fold_in(keys[3], 2), own, number, Q_DEV, N_DP, NEG, CAP, 2))(hard_owner_keys, hard_owner_turns).reshape((NQ, NEG))
    hard_row = plant(jax.random.randint(keys[4], (NQ, NEG), 0, NEG_DEV), jax.random.fold_in(keys[4], 1), 0, NEG_DEV - 1).astype(jnp.int32)
    return dict(queries=queries, passages=passages, negatives=negatives, hard_owner=hard_owner, hard_row=hard_row)


def score_weights(batch_scores, hard_scores, first_col):
    row_top = jnp.maximum(lax.optimization_barrier(jnp.max(batch_scores, axis=1)), lax.optimization_barrier(jnp.max(hard_scores, axis=1)))
    exp_total = lax.optimization_barrier(jnp.sum(jnp.exp(batch_scores - row_top[:, None]), axis=1)) + lax.optimization_barrier(jnp.sum(jnp.exp(hard_scores - row_top[:, None]), axis=1))
    log_total = row_top + jnp.log(exp_total)
    columns = jnp.arange(batch_scores.shape[1], dtype=jnp.int32)[None, :]
    targets = first_col + jnp.arange(batch_scores.shape[0], dtype=jnp.int32)[:, None]
    positive = (columns == targets).astype(jnp.float32)
    batch_weights = (jnp.exp(batch_scores - log_total[:, None]) - positive).astype(jnp.bfloat16)
    hard_weights = jnp.exp(hard_scores - log_total[:, None]).astype(jnp.bfloat16)
    return (batch_weights, hard_weights)

def reference(queries, passages, negatives, hard_owner, hard_row):
    score_scale = 3.0 / math.sqrt(D)
    batch_scores = jnp.dot(queries, passages.T, preferred_element_type=jnp.float32) * score_scale
    neg_index = (hard_owner * NEG_DEV + hard_row).astype(jnp.int32)
    query_float = queries.astype(jnp.float32)
    hard_list = []
    for column in range(NEG):
        picked = negatives[neg_index[:, column]].astype(jnp.float32)
        hard_list.append(lax.optimization_barrier(jnp.sum(query_float * picked, axis=1)))
    hard_scores = jnp.stack(hard_list, axis=1) * score_scale
    batch_weights, hard_weights = score_weights(batch_scores, hard_scores, 0)
    hard_float = hard_weights.astype(jnp.float32)
    query_acc = jnp.dot(batch_weights, passages, preferred_element_type=jnp.float32)
    neg_acc = jnp.zeros((NEG_DEV * N_DP, D), jnp.float32)
    for column in range(NEG):
        picked = negatives[neg_index[:, column]].astype(jnp.float32)
        query_acc = query_acc + hard_float[:, column:column + 1] * picked
        neg_terms = (hard_float[:, column:column + 1] * query_float).astype(jnp.bfloat16)
        neg_acc = neg_acc.at[neg_index[:, column]].add(neg_terms.astype(jnp.float32))
    passage_acc = jnp.dot(batch_weights.T, queries, preferred_element_type=jnp.float32)
    return (query_acc.astype(jnp.bfloat16), passage_acc.astype(jnp.bfloat16), neg_acc.astype(jnp.bfloat16))
```

```python
import math

import jax
import jax.numpy as jnp
from jax import lax
from jax.experimental import pallas as pl
from jax.experimental.pallas import tpu as pltpu
from jax.sharding import Mesh
from jax.sharding import PartitionSpec as P

BF16 = jnp.bfloat16
F32 = jnp.float32
NZ = 16
NB = 4
ABSENT = -1e30
VMEM_LIMIT = 48 * 1024 * 1024


def call(kernel, out_shapes, *args, smem=0, scratch=()):
    specs = [pl.BlockSpec(memory_space=pltpu.SMEM)] * smem
    specs += [pl.BlockSpec(memory_space=pltpu.VMEM)] * (len(args) - smem)
    return pl.pallas_call(
        kernel,
        out_shape=[jax.ShapeDtypeStruct(shape, dtype) for shape, dtype in out_shapes],
        in_specs=specs,
        out_specs=[pl.BlockSpec(memory_space=pltpu.VMEM)] * len(out_shapes),
        scratch_shapes=list(scratch),
        compiler_params=pltpu.CompilerParams(vmem_limit_bytes=VMEM_LIMIT),
    )(*args)


def pack_kernel(place, queries, passages, negatives, owners, rows, sent, columns):
    yh, z, c = place[0], place[1], place[2]
    width = queries.shape[1]
    line = lax.broadcasted_iota(jnp.int32, (NZ * 16, 128), 0)
    lane = lax.broadcasted_iota(jnp.int32, (NZ * 16, 128), 1)
    block = line % 16
    owner = (yh ^ (block // 2)) * (2 * NZ) + (line // 16) * 2 + (c ^ (block % 2))
    owner = jnp.where((block < NB) & (lane // 32 == z % 4), owner, -2)
    asked = jnp.full((NZ * 16, 128), -1, jnp.int32)
    for k in range(owners.shape[0]):
        asked = jnp.where(owners[k : k + 1, :] == owner, rows[k : k + 1, :], asked)
    asked = asked.astype(F32).astype(BF16)
    pieces = [queries[:, l * 128 : (l + 1) * 128] for l in range(width // 128)]
    for to in range(NZ):
        for l, piece in enumerate(pieces):
            sent[to, l * 32 : (l + 1) * 32, :] = piece
        sent[to, 128:144, :] = asked[to * 16 : (to + 1) * 16, :]
    columns[0:32, :] = passages[...]
    columns[32:256, :] = negatives[...]


def score_kernel(came, col0, col1, col2, col3, parts, queries, asked):
    scale = 3.0 / math.sqrt(4096)
    for z in range(NZ):
        for l in range(4):
            queries[z * 32 : (z + 1) * 32, l * 128 : (l + 1) * 128] = came[z, l * 32 : (l + 1) * 32, :]
    for g in range(4):
        rows = came[4 * g, 128:144, :].astype(F32)
        for z in range(4 * g + 1, 4 * g + 4):
            rows = jnp.maximum(rows, came[z, 128:144, :].astype(F32))
        asked[:, g * 128 : (g + 1) * 128] = rows[0:8, :].astype(jnp.int32)
    every = queries[...]
    place = lax.broadcasted_iota(jnp.int32, (224, 512), 0)
    for o, cols in enumerate((col0, col1, col2, col3)):
        part = lax.dot_general(cols[...], every, (((1,), (1,)), ((), ())), preferred_element_type=F32)
        want = asked[o : o + 1, :]
        hard = jnp.sum(jnp.where(place == want, part[32:256, :], 0.0), axis=0, keepdims=True) * scale
        hard = jnp.where(want >= 0, hard, ABSENT)
        h, a = o // 2, o % 2
        for l in range(4):
            lanes = slice(l * 128, (l + 1) * 128)
            parts[h * 4 + l, a * 32 : (a + 1) * 32, :] = part[0:32, lanes] * scale
            parts[h * 4 + l, 64 + a : 65 + a, :] = hard[:, lanes]
            if a == 1:
                parts[h * 4 + l, 66:72, :] = jnp.zeros((6, 128), F32)


def add_kernel(came, sent):
    total = came[0]
    for i in range(1, 8):
        total = total + came[i]
    for i in range(8):
        sent[i] = total


def stat_kernel(scores, sent):
    for l in range(4):
        batch = [scores[h * 4 + l, 0:64, :] for h in range(2)]
        hard = [scores[h * 4 + l, 64:66, :] for h in range(2)]
        top = jnp.maximum(
            jnp.max(jnp.maximum(batch[0], batch[1]), axis=0, keepdims=True),
            jnp.max(jnp.maximum(hard[0], hard[1]), axis=0, keepdims=True),
        )
        total = jnp.sum(jnp.exp(batch[0] - top) + jnp.exp(batch[1] - top), axis=0, keepdims=True)
        total = total + jnp.sum(jnp.exp(hard[0] - top) + jnp.exp(hard[1] - top), axis=0, keepdims=True)
        for to in range(NZ):
            sent[to, l : l + 1, :] = top
            sent[to, 4 + l : 5 + l, :] = total


def grad_kernel(place, stats, scores, asked, queries, col0, col1, col2, col3, q_part, keep, give, q_acc):
    z = place[1]
    logs = []
    for l in range(4):
        tops = stats[:, l, :]
        top = jnp.max(tops, axis=0, keepdims=True)
        total = jnp.sum(stats[:, 4 + l, :] * jnp.exp(tops - top), axis=0, keepdims=True)
        logs.append(top + jnp.log(total))
    log_total = jnp.concatenate(logs, axis=1)
    every = queries[...]
    line = lax.broadcasted_iota(jnp.int32, (224, 512), 0)
    row = lax.broadcasted_iota(jnp.int32, (32, 512), 0)
    lane = lax.broadcasted_iota(jnp.int32, (32, 512), 1)
    for o, cols in enumerate((col0, col1, col2, col3)):
        h, a = o // 2, o % 2
        batch = jnp.concatenate([scores[h * 4 + l, a * 32 : (a + 1) * 32, :] for l in range(4)], axis=1)
        hard = jnp.concatenate([scores[h * 4 + l, 64 + a : 65 + a, :] for l in range(4)], axis=1)
        weights = jnp.exp(batch - log_total)
        if o == 0:
            weights = weights - (lane == z * 32 + row).astype(F32)
        hard = jnp.exp(hard - log_total)
        hard = jnp.where(line == asked[o : o + 1, :], hard, 0.0)
        both = jnp.concatenate([weights.astype(BF16), hard.astype(BF16)], axis=0)
        col_grad = jnp.dot(both, every, preferred_element_type=F32).astype(BF16)
        (give if a else keep)[h] = col_grad
        term = lax.dot_general(both, cols[...], (((0,), (0,)), ((), ())), preferred_element_type=F32)
        if o == 0:
            q_acc[...] = term
        elif o < NB - 1:
            q_acc[...] += term
        else:
            q_part[...] = (q_acc[...] + term).astype(BF16).reshape(NZ, 32, 512)


def pair_kernel(keep, came, own, sent):
    own[...] = keep[0].astype(F32) + came[0].astype(F32)
    sent[...] = (keep[1].astype(F32) + came[1].astype(F32)).astype(BF16)


def column_kernel(own, came, passage_out, negative_out):
    passage_out[...] = (own[0:32, :] + came[0:32, :].astype(F32)).astype(BF16)
    negative_out[...] = (own[32:256, :] + came[32:256, :].astype(F32)).astype(BF16)


def query_kernel(came, query_out):
    total = came[0].astype(F32)
    for z in range(1, NZ):
        total = total + came[z].astype(F32)
    query_out[...] = total.astype(BF16)


def swap(x, axis):
    return lax.ppermute(x, axis, [(0, 1), (1, 0)])


def exchange(x, axis):
    return lax.all_to_all(x, axis, split_axis=0, concat_axis=0, tiled=True)


def shards(queries, passages, negatives, hard_owner, hard_row):
    place = jnp.stack([lax.axis_index("yh"), lax.axis_index("z"), lax.axis_index("c")]).astype(jnp.int32)
    owners = jnp.tile(hard_owner.T, (1, 4))
    rows = jnp.tile(hard_row.T, (1, 4))
    sent, col0 = call(
        pack_kernel, [((NZ, 144, 128), BF16), ((256, 512), BF16)],
        place, queries, passages, negatives, owners, rows, smem=1,
    )
    col2 = swap(col0, "yh")
    col1 = swap(col0, "c")
    col3 = swap(col2, "c")
    came = exchange(sent, "z")
    parts, every, asked = call(
        score_kernel, [((8, 72, 128), F32), ((512, 512), BF16), ((8, 512), jnp.int32)],
        came, col0, col1, col2, col3,
    )
    (summed,) = call(add_kernel, [((8, 72, 128), F32)], exchange(parts, ("yl", "x")))
    scores = exchange(summed, ("yl", "x"))
    (stats,) = call(stat_kernel, [((NZ, 8, 128), F32)], scores)
    stats = exchange(stats, "z")
    q_part, keep, give = call(
        grad_kernel, [((NZ, 32, 512), BF16), ((2, 256, 512), BF16), ((2, 256, 512), BF16)],
        place, stats, scores, asked, every, col0, col1, col2, col3,
        smem=1, scratch=[pltpu.VMEM((512, 512), F32)],
    )
    own, cross = call(pair_kernel, [((256, 512), F32), ((256, 512), BF16)], keep, swap(give, "c"))
    cross = swap(cross, "yh")
    q_came = exchange(q_part, "z")
    passage_out, negative_out = call(column_kernel, [((32, 512), BF16), ((224, 512), BF16)], own, cross)
    (query_out,) = call(query_kernel, [((32, 512), BF16)], q_came)
    return (query_out, passage_out, negative_out)


def solution(mesh):
    fine = Mesh(mesh.devices.reshape(2, NZ, 2, 2, 4), ("yh", "z", "c", "yl", "x"))
    dp, mp = ("yh", "z", "c"), ("yl", "x")
    return jax.shard_map(
        shards,
        mesh=fine,
        in_specs=(P(dp, mp), P(dp, mp), P(dp, mp), P(dp, None), P(dp, None)),
        out_specs=(P(dp, mp), P(dp, mp), P(dp, mp)),
        check_vma=False,
    )
```

```python
import math

import jax
import jax.numpy as jnp
from jax import lax
from jax.experimental import pallas as pl
from jax.experimental.pallas import tpu as pltpu
from jax.sharding import Mesh
from jax.sharding import PartitionSpec as P

BF16 = jnp.bfloat16
F32 = jnp.float32
NZ = 8
NB = 8
ROWS = 256
GROUPS = ROWS // 128
ABSENT = -1e30
VMEM_LIMIT = 48 * 1024 * 1024


def call(kernel, out_shapes, *args, smem=0, hbm=0, scratch=()):
    specs = [pl.BlockSpec(memory_space=pltpu.SMEM)] * smem
    specs += [pl.BlockSpec(memory_space=pltpu.HBM)] * hbm
    specs += [pl.BlockSpec(memory_space=pltpu.VMEM)] * (len(args) - smem - hbm)
    return pl.pallas_call(
        kernel,
        out_shape=[jax.ShapeDtypeStruct(shape, dtype) for shape, dtype in out_shapes],
        in_specs=specs,
        out_specs=[pl.BlockSpec(memory_space=pltpu.VMEM)] * len(out_shapes),
        scratch_shapes=list(scratch),
        compiler_params=pltpu.CompilerParams(vmem_limit_bytes=VMEM_LIMIT),
    )(*args)


def pack_kernel(place, queries, passages, negatives, owners, rows, sent, columns, mine, short, wide, sems):
    copies = [
        pltpu.make_async_copy(owners, short.at[0], sems.at[0]),
        pltpu.make_async_copy(rows, short.at[1], sems.at[1]),
        pltpu.make_async_copy(queries, mine, sems.at[2]),
        pltpu.make_async_copy(negatives, columns.at[32:256], sems.at[3]),
        pltpu.make_async_copy(passages, columns.at[0:32], sems.at[4]),
    ]
    for copy in copies:
        copy.start()
    yh, zh, zp, c = place[0], place[1], place[2], place[3]
    line = lax.broadcasted_iota(jnp.int32, (NZ * 16, 128), 0)
    lane = lax.broadcasted_iota(jnp.int32, (NZ * 16, 128), 1)
    block = line % 16
    z = (line // 16) * 2 + (zp ^ (block // 4))
    owner = ((yh ^ (block // 2 % 2)) * (2 * NZ) + z) * 2 + (c ^ (block % 2))
    owner = jnp.where((block < NB) & (lane // 32 == zh % 4), owner, -2)
    copies[0].wait()
    copies[1].wait()
    for j in range(4):
        wide[:, :, j * 32 : (j + 1) * 32] = short[...]
    asked = jnp.full((NZ * 16, 128), -1, jnp.int32)
    for k in range(short.shape[1]):
        asked = jnp.where(wide[0, k : k + 1, :] == owner, wide[1, k : k + 1, :], asked)
    asked = asked.astype(F32).astype(BF16)
    for to in range(NZ):
        sent[to, 128:144, :] = asked[to * 16 : (to + 1) * 16, :]
    copies[2].wait()
    for to in range(NZ):
        for l in range(4):
            sent[to, l * 32 : (l + 1) * 32, :] = mine[:, l * 128 : (l + 1) * 128]
    copies[3].wait()
    copies[4].wait()


def score_kernel(came, *refs):
    columns, (parts, queries, asked) = refs[:NB], refs[NB:]
    scale = 3.0 / math.sqrt(4096)
    for z in range(NZ):
        for l in range(4):
            queries[z * 32 : (z + 1) * 32, l * 128 : (l + 1) * 128] = came[z, l * 32 : (l + 1) * 32, :]
    for g in range(GROUPS):
        rows = came[4 * g, 128:144, :].astype(F32)
        for z in range(4 * g + 1, 4 * g + 4):
            rows = jnp.maximum(rows, came[z, 128:144, :].astype(F32))
        asked[:, g * 128 : (g + 1) * 128] = rows[0:NB, :].astype(jnp.int32)
    every = queries[...]
    place = lax.broadcasted_iota(jnp.int32, (224, ROWS), 0)
    for o in range(NB):
        part = lax.dot_general(columns[o][...], every, (((1,), (1,)), ((), ())), preferred_element_type=F32)
        want = asked[o : o + 1, :]
        hard = jnp.sum(jnp.where(place == want, part[32:256, :], 0.0), axis=0, keepdims=True) * scale
        hard = jnp.where(want >= 0, hard, ABSENT)
        h, a = o // 2, o % 2
        for l in range(GROUPS):
            lanes = slice(l * 128, (l + 1) * 128)
            parts[h * GROUPS + l, a * 32 : (a + 1) * 32, :] = part[0:32, lanes] * scale
            parts[h * GROUPS + l, 64 + a : 65 + a, :] = hard[:, lanes]
            if a == 1:
                parts[h * GROUPS + l, 66:72, :] = jnp.zeros((6, 128), F32)


def add_kernel(came, sent):
    total = came[0]
    for i in range(1, 8):
        total = total + came[i]
    for i in range(8):
        sent[i] = total


def stat_kernel(scores, sent):
    for l in range(GROUPS):
        batch = [scores[h * GROUPS + l, 0:64, :] for h in range(NB // 2)]
        hard = [scores[h * GROUPS + l, 64:66, :] for h in range(NB // 2)]
        top = jnp.maximum(
            jnp.max(jnp.maximum(jnp.maximum(batch[0], batch[1]), jnp.maximum(batch[2], batch[3])), axis=0, keepdims=True),
            jnp.max(jnp.maximum(jnp.maximum(hard[0], hard[1]), jnp.maximum(hard[2], hard[3])), axis=0, keepdims=True),
        )
        total = jnp.sum(sum(jnp.exp(b - top) for b in batch), axis=0, keepdims=True)
        total = total + jnp.sum(sum(jnp.exp(h - top) for h in hard), axis=0, keepdims=True)
        for to in range(NZ):
            sent[to, l : l + 1, :] = top
            sent[to, GROUPS + l : GROUPS + l + 1, :] = total
    for to in range(NZ):
        sent[to, 2 * GROUPS : 8, :] = jnp.zeros((8 - 2 * GROUPS, 128), F32)


def grad_kernel(place, stats, scores, asked, queries, *refs):
    columns, (q_part, keep, give, q_acc) = refs[:NB], refs[NB:]
    zh = place[1]
    logs = []
    for l in range(GROUPS):
        tops = stats[:, l, :]
        top = jnp.max(tops, axis=0, keepdims=True)
        total = jnp.sum(stats[:, GROUPS + l, :] * jnp.exp(tops - top), axis=0, keepdims=True)
        logs.append(top + jnp.log(total))
    log_total = jnp.concatenate(logs, axis=1)
    every = queries[...]
    line = lax.broadcasted_iota(jnp.int32, (224, ROWS), 0)
    row = lax.broadcasted_iota(jnp.int32, (32, ROWS), 0)
    lane = lax.broadcasted_iota(jnp.int32, (32, ROWS), 1)
    for o in range(NB):
        h, a = o // 2, o % 2
        batch = jnp.concatenate([scores[h * GROUPS + l, a * 32 : (a + 1) * 32, :] for l in range(GROUPS)], axis=1)
        hard = jnp.concatenate([scores[h * GROUPS + l, 64 + a : 65 + a, :] for l in range(GROUPS)], axis=1)
        weights = jnp.exp(batch - log_total)
        if o == 0:
            weights = weights - (lane == zh * 32 + row).astype(F32)
        hard = jnp.exp(hard - log_total)
        hard = jnp.where(line == asked[o : o + 1, :], hard, 0.0)
        both = jnp.concatenate([weights.astype(BF16), hard.astype(BF16)], axis=0)
        (give if a else keep)[h] = jnp.dot(both, every, preferred_element_type=F32).astype(BF16)
        term = lax.dot_general(both, columns[o][...], (((0,), (0,)), ((), ())), preferred_element_type=F32)
        if o == 0:
            q_acc[...] = term
        elif o < NB - 1:
            q_acc[...] += term
        else:
            q_part[...] = (q_acc[...] + term).astype(BF16).reshape(NZ, 32, 512)


def pair_kernel(keep, came, own, *sent):
    own[...] = keep[0].astype(F32) + came[0].astype(F32)
    for h in range(1, NB // 2):
        sent[h - 1][...] = (keep[h].astype(F32) + came[h].astype(F32)).astype(BF16)


def column_kernel(own, *refs):
    came, (passage_out, negative_out) = refs[: NB // 2 - 1], refs[NB // 2 - 1 :]
    for out, rows in ((passage_out, slice(0, 32)), (negative_out, slice(32, 256))):
        total = own[rows, :]
        for other in came:
            total = total + other[rows, :].astype(F32)
        out[...] = total.astype(BF16)


def query_kernel(came, query_out):
    total = came[0].astype(F32)
    for z in range(1, NZ):
        total = total + came[z].astype(F32)
    query_out[...] = total.astype(BF16)


def swap(x, axes):
    size = 2 ** len(axes)
    return lax.ppermute(x, axes, [(i, size - 1 - i) for i in range(size)])


def exchange(x, axes):
    return lax.all_to_all(x, axes, split_axis=0, concat_axis=0, tiled=True)


def shards(queries, passages, negatives, hard_owner, hard_row):
    place = jnp.stack([lax.axis_index(axis) for axis in ("yh", "zh", "zp", "c")]).astype(jnp.int32)
    sent, own = call(
        pack_kernel, [((NZ, 144, 128), BF16), ((256, 512), BF16)],
        place, queries, passages, negatives, hard_owner.T, hard_row.T, smem=1, hbm=5,
        scratch=[
            pltpu.VMEM((32, 512), BF16), pltpu.VMEM((2, 7, 32), jnp.int32), pltpu.VMEM((2, 7, 128), jnp.int32),
            pltpu.SemaphoreType.DMA((5,)),
        ],
    )
    came = exchange(sent, "zh")
    others = [own, swap(own, ("yh",)), swap(own, ("zp",)), swap(own, ("yh", "zp"))]
    columns = [block for other in others for block in (other, swap(other, ("c",)))]
    parts, every, asked = call(
        score_kernel, [((8, 72, 128), F32), ((ROWS, 512), BF16), ((NB, ROWS), jnp.int32)], came, *columns
    )
    (summed,) = call(add_kernel, [((8, 72, 128), F32)], exchange(parts, ("yl", "x")))
    scores = exchange(summed, ("yl", "x"))
    (stats,) = call(stat_kernel, [((NZ, 8, 128), F32)], scores)
    stats = exchange(stats, "zh")
    q_part, keep, give = call(
        grad_kernel, [((NZ, 32, 512), BF16), ((NB // 2, 256, 512), BF16), ((NB // 2, 256, 512), BF16)],
        place, stats, scores, asked, every, *columns, smem=1, scratch=[pltpu.VMEM((ROWS, 512), F32)],
    )
    mine, by_yh, by_zp, by_both = call(
        pair_kernel, [((256, 512), F32)] + [((256, 512), BF16)] * 3, keep, swap(give, ("c",))
    )
    q_came = exchange(q_part, "zh")
    passage_out, negative_out = call(
        column_kernel, [((32, 512), BF16), ((224, 512), BF16)],
        mine, swap(by_both, ("yh", "zp")), swap(by_yh, ("yh",)), swap(by_zp, ("zp",)),
    )
    (query_out,) = call(query_kernel, [((32, 512), BF16)], q_came)
    return (query_out, passage_out, negative_out)


def solution(mesh):
    fine = Mesh(mesh.devices.reshape(2, NZ, 2, 2, 2, 4), ("yh", "zh", "zp", "c", "yl", "x"))
    dp, mp = ("yh", "zh", "zp", "c"), ("yl", "x")
    return jax.shard_map(
        shards,
        mesh=fine,
        in_specs=(P(dp, mp), P(dp, mp), P(dp, mp), P(dp, None), P(dp, None)),
        out_specs=(P(dp, mp), P(dp, mp), P(dp, mp)),
        check_vma=False,
    )
```

```python
import math

import jax
import jax.numpy as jnp
from jax import lax
from jax.experimental import pallas as pl
from jax.experimental.pallas import tpu as pltpu
from jax.sharding import Mesh
from jax.sharding import PartitionSpec as P

BF16 = jnp.bfloat16
F32 = jnp.float32
NZ = 16
NH = 8
NB = 4
ROWS = 512
ABSENT = -1e30
VMEM_LIMIT = 48 * 1024 * 1024
PACK_LIMIT = 62 * 1024 * 1024


def call(kernel, out_shapes, *args, smem=0, hbm=0, scratch=(), limit=VMEM_LIMIT):
    specs = [pl.BlockSpec(memory_space=pltpu.SMEM)] * smem
    specs += [pl.BlockSpec(memory_space=pl.ANY)] * hbm
    specs += [pl.BlockSpec(memory_space=pltpu.VMEM)] * (len(args) - smem - hbm)
    return pl.pallas_call(
        kernel,
        out_shape=[jax.ShapeDtypeStruct(shape, dtype) for shape, dtype in out_shapes],
        in_specs=specs,
        out_specs=[pl.BlockSpec(memory_space=pltpu.VMEM)] * len(out_shapes),
        scratch_shapes=list(scratch),
        compiler_params=pltpu.CompilerParams(vmem_limit_bytes=limit),
    )(*args)


def pack_kernel(place, queries, owners, rows, sent, mine, short, wide, sems):
    copies = [
        pltpu.make_async_copy(owners, short.at[0], sems.at[0]),
        pltpu.make_async_copy(rows, short.at[1], sems.at[1]),
        pltpu.make_async_copy(queries, mine, sems.at[2]),
    ]
    for copy in copies:
        copy.start()
    yh, zh, zp, c = place[0], place[1], place[2], place[3]
    line = lax.broadcasted_iota(jnp.int32, (NH * 16, 128), 0)
    lane = lax.broadcasted_iota(jnp.int32, (NH * 16, 128), 1)
    block = line % 16
    z = (line // 16) * 2 + (zp ^ (block // 4))
    owner = ((yh ^ (block // 2 % 2)) * NZ + z) * 2 + (c ^ (block % 2))
    owner = jnp.where((block < 2 * NB) & (lane // 32 == zh % 4), owner, -2)
    copies[0].wait()
    copies[1].wait()
    for j in range(4):
        wide[:, :, j * 32 : (j + 1) * 32] = short[...]
    asked = jnp.full((NH * 16, 128), -1, jnp.int32)
    for k in range(short.shape[1]):
        asked = jnp.where(wide[0, k : k + 1, :] == owner, wide[1, k : k + 1, :], asked)
    asked = asked.astype(F32).astype(BF16)
    for to in range(NH):
        sent[to, 128:144, :] = asked[to * 16 : (to + 1) * 16, :]
    copies[2].wait()
    for to in range(NH):
        for l in range(4):
            sent[to, l * 32 : (l + 1) * 32, :] = mine[:, l * 128 : (l + 1) * 128]


def column_pack_kernel(passages, negatives, columns, sems):
    copies = [
        pltpu.make_async_copy(negatives, columns.at[32:256], sems.at[0]),
        pltpu.make_async_copy(passages, columns.at[0:32], sems.at[1]),
    ]
    for copy in copies:
        copy.start()
    for copy in copies:
        copy.wait()


def score_kernel(near, far, col0, col1, col2, col3, parts, queries, asked):
    scale = 3.0 / math.sqrt(4096)
    for s, came in enumerate((near, far)):
        for z in range(NH):
            for l in range(4):
                rows = slice((s * NH + z) * 32, (s * NH + z + 1) * 32)
                queries[rows, l * 128 : (l + 1) * 128] = came[z, l * 32 : (l + 1) * 32, :]
        for g in range(2):
            rows = came[4 * g, 128:144, :].astype(F32)
            for z in range(4 * g + 1, 4 * g + 4):
                rows = jnp.maximum(rows, came[z, 128:144, :].astype(F32))
            rows = rows[s * NB : (s + 1) * NB, :].astype(jnp.int32)
            asked[0:NB, (2 * s + g) * 128 : (2 * s + g + 1) * 128] = rows
    asked[NB:8, :] = jnp.full((8 - NB, ROWS), -1, jnp.int32)
    every = queries[...]
    place = lax.broadcasted_iota(jnp.int32, (224, ROWS), 0)
    for o, cols in enumerate((col0, col1, col2, col3)):
        part = lax.dot_general(cols[...], every, (((1,), (1,)), ((), ())), preferred_element_type=F32)
        want = asked[o : o + 1, :]
        hard = jnp.sum(jnp.where(place == want, part[32:256, :], 0.0), axis=0, keepdims=True) * scale
        hard = jnp.where(want >= 0, hard, ABSENT)
        h, a = o // 2, o % 2
        for l in range(4):
            lanes = slice(l * 128, (l + 1) * 128)
            parts[h * 4 + l, a * 32 : (a + 1) * 32, :] = part[0:32, lanes] * scale
            parts[h * 4 + l, 64 + a : 65 + a, :] = hard[:, lanes]
            if a == 1:
                parts[h * 4 + l, 66:72, :] = jnp.zeros((6, 128), F32)


def add_kernel(came, sent):
    total = came[0]
    for i in range(1, 8):
        total = total + came[i]
    for i in range(8):
        sent[i] = total


def stat_kernel(place, scores, sent, tops):
    zp = place[2]
    pairs = []
    for l in range(4):
        batch = [scores[h * 4 + l, 0:64, :] for h in range(2)]
        hard = [scores[h * 4 + l, 64:66, :] for h in range(2)]
        top = jnp.maximum(
            jnp.max(jnp.maximum(batch[0], batch[1]), axis=0, keepdims=True),
            jnp.max(jnp.maximum(hard[0], hard[1]), axis=0, keepdims=True),
        )
        total = jnp.sum(jnp.exp(batch[0] - top) + jnp.exp(batch[1] - top), axis=0, keepdims=True)
        total = total + jnp.sum(jnp.exp(hard[0] - top) + jnp.exp(hard[1] - top), axis=0, keepdims=True)
        pairs.append((top, total))
    tops[...] = jnp.concatenate([top for top, _ in pairs], axis=1)
    for l in range(4):
        for k in range(2):
            row = jnp.where(zp == 0, pairs[l][k], pairs[l ^ 2][k])
            for to in range(NZ):
                sent[to, 4 * k + l : 4 * k + l + 1, :] = row


def block_scores(scores, o):
    h, a = o // 2, o % 2
    batch = jnp.concatenate([scores[h * 4 + l, a * 32 : (a + 1) * 32, :] for l in range(4)], axis=1)
    hard = jnp.concatenate([scores[h * 4 + l, 64 + a : 65 + a, :] for l in range(4)], axis=1)
    return batch, hard


def block_weights(batch, hard, want):
    line = lax.broadcasted_iota(jnp.int32, (224, ROWS), 0)
    hard = jnp.where(line == want, hard, 0.0)
    return jnp.concatenate([batch.astype(BF16), hard.astype(BF16)], axis=0)


def is_target(zh):
    row = lax.broadcasted_iota(jnp.int32, (32, ROWS), 0)
    lane = lax.broadcasted_iota(jnp.int32, (32, ROWS), 1)
    return lane == zh * 32 + row


def share_kernel(place, scores, tops, asked, col0, col1, col2, col3, keep, give, q_acc):
    top = tops[...]
    for o, cols in enumerate((col0, col1, col2, col3)):
        batch, hard = block_scores(scores, o)
        weights = jnp.exp(batch - top)
        if o == 0:
            weights = jnp.where(is_target(place[1]), 0.0, weights)
        both = block_weights(weights, jnp.exp(hard - top), asked[o : o + 1, :])
        term = lax.dot_general(both, cols[...], (((0,), (0,)), ((), ())), preferred_element_type=F32)
        if o == 0:
            q_acc[...] = term
        elif o < NB - 1:
            q_acc[...] += term
        else:
            total = (q_acc[...] + term).astype(BF16)
            keep[...] = total[0:256, :]
            give[...] = total[256:512, :]


def join_kernel(place, stats, keep, came, sent, logs):
    z, zp = place[1] * 2 + place[2], place[2]
    absolute = []
    for l in range(4):
        tops = stats[:, l, :]
        top = jnp.max(tops, axis=0, keepdims=True)
        absolute.append(top + jnp.log(jnp.sum(stats[:, 4 + l, :] * jnp.exp(tops - top), axis=0, keepdims=True)))
    mine = stats[z]
    other = stats[z ^ 1]
    relative = [jnp.where(zp == 0, absolute[l], absolute[l ^ 2]) for l in range(4)]
    logs[...] = jnp.concatenate(relative, axis=1)
    rows = []
    for tops in (mine, other):
        for l in range(2):
            rows.append(jnp.exp(jnp.where(zp == 0, tops[l : l + 1, :], tops[l + 2 : l + 3, :]) - relative[l]))
    factors = jnp.concatenate(rows + [jnp.zeros((124, 128), F32)], axis=0).T
    for l in range(2):
        lines = slice(l * 128, (l + 1) * 128)
        total = keep[lines, :].astype(F32) * factors[:, l : l + 1] + came[lines, :].astype(F32) * factors[:, 2 + l : 3 + l]
        sent[l * 4 : (l + 1) * 4] = total.astype(BF16).reshape(4, 32, 512)


def column_grad_kernel(place, logs, scores, asked, queries, keep, give, at_target):
    log_total = logs[...]
    every = queries[...]
    for o in range(NB):
        batch, hard = block_scores(scores, o)
        weights = jnp.exp(batch - log_total)
        if o == 0:
            target = is_target(place[1])
            weights = jnp.where(target, weights - 1.0, weights)
            own = jnp.sum(jnp.where(target, weights, 0.0), axis=1, keepdims=True)
            at_target[...] = jnp.broadcast_to(own.astype(BF16).astype(F32), (32, 128))
        both = block_weights(weights, jnp.exp(hard - log_total), asked[o : o + 1, :])
        (give if o % 2 else keep)[o // 2] = jnp.dot(both, every, preferred_element_type=F32).astype(BF16)


def pair_kernel(keep, came, own, sent):
    own[...] = keep[0].astype(F32) + came[0].astype(F32)
    sent[...] = (keep[1].astype(F32) + came[1].astype(F32)).astype(BF16)


def column_kernel(own, came, passage_out, negative_out):
    passage_out[...] = (own[0:32, :] + came[0:32, :].astype(F32)).astype(BF16)
    negative_out[...] = (own[32:256, :] + came[32:256, :].astype(F32)).astype(BF16)


def query_kernel(came, at_target, passages, query_out):
    total = at_target[:, 0:1] * passages[...].astype(F32)
    for z in range(NH):
        total = total + came[z].astype(F32)
    query_out[...] = total.astype(BF16)


def swap(x, axis):
    return lax.ppermute(x, axis, [(0, 1), (1, 0)])


def exchange(x, axes):
    return lax.all_to_all(x, axes, split_axis=0, concat_axis=0, tiled=True)


def shards(queries, passages, negatives, hard_owner, hard_row):
    place = jnp.stack([lax.axis_index(axis) for axis in ("yh", "zh", "zp", "c")]).astype(jnp.int32)
    (sent,) = call(
        pack_kernel, [((NH, 144, 128), BF16)],
        place, queries, hard_owner.T, hard_row.T, smem=1, hbm=3, limit=PACK_LIMIT,
        scratch=[
            pltpu.VMEM((32, 512), BF16), pltpu.VMEM((2, 7, 32), jnp.int32), pltpu.VMEM((2, 7, 128), jnp.int32),
            pltpu.SemaphoreType.DMA((3,)),
        ],
    )
    near = exchange(sent, "zh")
    far = swap(near, "zp")
    (col0,) = call(
        column_pack_kernel, [((256, 512), BF16)], passages, negatives, hbm=2, limit=PACK_LIMIT,
        scratch=[pltpu.SemaphoreType.DMA((2,))],
    )
    col2 = swap(col0, "yh")
    col1 = swap(col0, "c")
    col3 = swap(col2, "c")
    parts, every, asked = call(
        score_kernel, [((8, 72, 128), F32), ((ROWS, 512), BF16), ((8, ROWS), jnp.int32)],
        near, far, col0, col1, col2, col3,
    )
    (summed,) = call(add_kernel, [((8, 72, 128), F32)], exchange(parts, ("yl", "x")))
    scores = exchange(summed, ("yl", "x"))
    stats, tops = call(stat_kernel, [((NZ, 8, 128), F32), ((1, ROWS), F32)], place, scores, smem=1)
    stats = exchange(stats, ("zh", "zp"))
    q_keep, q_give = call(
        share_kernel, [((256, 512), BF16), ((256, 512), BF16)],
        place, scores, tops, asked, col0, col1, col2, col3, smem=1, scratch=[pltpu.VMEM((ROWS, 512), F32)],
    )
    q_pair, logs = call(
        join_kernel, [((NH, 32, 512), BF16), ((1, ROWS), F32)], place, stats, q_keep, swap(q_give, "zp"), smem=1
    )
    q_came = exchange(q_pair, "zh")
    keep, give, at_target = call(
        column_grad_kernel, [((2, 256, 512), BF16), ((2, 256, 512), BF16), ((32, 128), F32)],
        place, logs, scores, asked, every, smem=1,
    )
    own, cross = call(pair_kernel, [((256, 512), F32), ((256, 512), BF16)], keep, swap(give, "c"))
    cross = swap(cross, "yh")
    passage_out, negative_out = call(column_kernel, [((32, 512), BF16), ((224, 512), BF16)], own, cross)
    (query_out,) = call(query_kernel, [((32, 512), BF16)], q_came, at_target, passages)
    return (query_out, passage_out, negative_out)


def solution(mesh):
    fine = Mesh(mesh.devices.reshape(2, NH, 2, 2, 2, 4), ("yh", "zh", "zp", "c", "yl", "x"))
    dp, mp = ("yh", "zh", "zp", "c"), ("yl", "x")
    return jax.shard_map(
        shards,
        mesh=fine,
        in_specs=(P(dp, mp), P(dp, mp), P(dp, mp), P(dp, None), P(dp, None)),
        out_specs=(P(dp, mp), P(dp, mp), P(dp, mp)),
        check_vma=False,
    )
```

```python
import math

import jax
import jax.numpy as jnp
from jax import lax
from jax.experimental import pallas as pl
from jax.experimental.pallas import tpu as pltpu
from jax.sharding import Mesh
from jax.sharding import PartitionSpec as P

BF16 = jnp.bfloat16
F32 = jnp.float32
NZ = 16
NH = 8
NB = 4
ROWS = 512
ABSENT = -1e30
VMEM_LIMIT = 48 * 1024 * 1024
PACK_LIMIT = 62 * 1024 * 1024


def call(kernel, out_shapes, *args, hbm=0, scratch=(), limit=VMEM_LIMIT):
    specs = [pl.BlockSpec(memory_space=pl.ANY)] * hbm
    specs += [pl.BlockSpec(memory_space=pltpu.VMEM)] * (len(args) - hbm)
    return pl.pallas_call(
        kernel,
        out_shape=[jax.ShapeDtypeStruct(shape, dtype) for shape, dtype in out_shapes],
        in_specs=specs,
        out_specs=[pl.BlockSpec(memory_space=pltpu.VMEM)] * len(out_shapes),
        scratch_shapes=list(scratch),
        compiler_params=pltpu.CompilerParams(vmem_limit_bytes=limit),
    )(*args)


def pack_kernel(queries, owners, rows, sent, mine, short, wide, sems):
    copies = [
        pltpu.make_async_copy(owners, short.at[0], sems.at[0]),
        pltpu.make_async_copy(rows, short.at[1], sems.at[1]),
        pltpu.make_async_copy(queries, mine, sems.at[2]),
    ]
    for copy in copies:
        copy.start()
    yh, zh, zp, c = (lax.axis_index(axis) for axis in ("yh", "zh", "zp", "c"))
    line = lax.broadcasted_iota(jnp.int32, (NH * 16, 128), 0)
    lane = lax.broadcasted_iota(jnp.int32, (NH * 16, 128), 1)
    block = line % 16
    z = (line // 16) * 2 + (zp ^ (block // 4))
    owner = ((yh ^ (block // 2 % 2)) * NZ + z) * 2 + (c ^ (block % 2))
    owner = jnp.where((block < 2 * NB) & (lane // 32 == zh % 4), owner, -2)
    copies[0].wait()
    copies[1].wait()
    for j in range(4):
        wide[:, :, j * 32 : (j + 1) * 32] = short[...]
    asked = jnp.full((NH * 16, 128), -1, jnp.int32)
    for k in range(short.shape[1]):
        asked = jnp.where(wide[0, k : k + 1, :] == owner, wide[1, k : k + 1, :], asked)
    asked = asked.astype(F32).astype(BF16)
    for to in range(NH):
        sent[to, 128:144, :] = asked[to * 16 : (to + 1) * 16, :]
    copies[2].wait()
    for to in range(NH):
        for l in range(4):
            sent[to, l * 32 : (l + 1) * 32, :] = mine[:, l * 128 : (l + 1) * 128]


def column_pack_kernel(passages, negatives, columns, sems):
    copies = [
        pltpu.make_async_copy(negatives, columns.at[32:256], sems.at[0]),
        pltpu.make_async_copy(passages, columns.at[0:32], sems.at[1]),
    ]
    for copy in copies:
        copy.start()
    for copy in copies:
        copy.wait()


def score_kernel(near, far, col0, col1, col2, col3, parts, queries, asked):
    scale = 3.0 / math.sqrt(4096)
    for s, came in enumerate((near, far)):
        for z in range(NH):
            for l in range(4):
                rows = slice((s * NH + z) * 32, (s * NH + z + 1) * 32)
                queries[rows, l * 128 : (l + 1) * 128] = came[z, l * 32 : (l + 1) * 32, :]
        for g in range(2):
            rows = came[4 * g, 128:144, :].astype(F32)
            for z in range(4 * g + 1, 4 * g + 4):
                rows = jnp.maximum(rows, came[z, 128:144, :].astype(F32))
            rows = rows[s * NB : (s + 1) * NB, :].astype(jnp.int32)
            asked[0:NB, (2 * s + g) * 128 : (2 * s + g + 1) * 128] = rows
    asked[NB:8, :] = jnp.full((8 - NB, ROWS), -1, jnp.int32)
    every = queries[...]
    place = lax.broadcasted_iota(jnp.int32, (224, ROWS), 0)
    for o, cols in enumerate((col0, col1, col2, col3)):
        part = lax.dot_general(cols[...], every, (((1,), (1,)), ((), ())), preferred_element_type=F32)
        want = asked[o : o + 1, :]
        hard = jnp.sum(jnp.where(place == want, part[32:256, :], 0.0), axis=0, keepdims=True) * scale
        hard = jnp.where(want >= 0, hard, ABSENT)
        h, a = o // 2, o % 2
        for l in range(4):
            lanes = slice(l * 128, (l + 1) * 128)
            parts[h * 4 + l, a * 32 : (a + 1) * 32, :] = part[0:32, lanes] * scale
            parts[h * 4 + l, 64 + a : 65 + a, :] = hard[:, lanes]
            if a == 1:
                parts[h * 4 + l, 66:72, :] = jnp.zeros((6, 128), F32)


def add_kernel(came, sent):
    total = came[0]
    for i in range(1, 8):
        total = total + came[i]
    for i in range(8):
        sent[i] = total


def stat_kernel(scores, sent, tops):
    zp = lax.axis_index("zp")
    pairs = []
    for l in range(4):
        batch = [scores[h * 4 + l, 0:64, :] for h in range(2)]
        hard = [scores[h * 4 + l, 64:66, :] for h in range(2)]
        top = jnp.maximum(
            jnp.max(jnp.maximum(batch[0], batch[1]), axis=0, keepdims=True),
            jnp.max(jnp.maximum(hard[0], hard[1]), axis=0, keepdims=True),
        )
        total = jnp.sum(jnp.exp(batch[0] - top) + jnp.exp(batch[1] - top), axis=0, keepdims=True)
        total = total + jnp.sum(jnp.exp(hard[0] - top) + jnp.exp(hard[1] - top), axis=0, keepdims=True)
        pairs.append((top, total))
    tops[...] = jnp.concatenate([top for top, _ in pairs], axis=1)
    for l in range(4):
        for k in range(2):
            row = jnp.where(zp == 0, pairs[l][k], pairs[l ^ 2][k])
            for to in range(NZ):
                sent[to, 4 * k + l : 4 * k + l + 1, :] = row


def block_scores(scores, o):
    h, a = o // 2, o % 2
    batch = jnp.concatenate([scores[h * 4 + l, a * 32 : (a + 1) * 32, :] for l in range(4)], axis=1)
    hard = jnp.concatenate([scores[h * 4 + l, 64 + a : 65 + a, :] for l in range(4)], axis=1)
    return batch, hard


def block_weights(batch, hard, want):
    line = lax.broadcasted_iota(jnp.int32, (224, ROWS), 0)
    hard = jnp.where(line == want, hard, 0.0)
    return jnp.concatenate([batch.astype(BF16), hard.astype(BF16)], axis=0)


def is_target():
    zh = lax.axis_index("zh")
    row = lax.broadcasted_iota(jnp.int32, (32, ROWS), 0)
    lane = lax.broadcasted_iota(jnp.int32, (32, ROWS), 1)
    return lane == zh * 32 + row


def share_kernel(scores, tops, asked, col0, col1, col2, col3, keep, *refs):
    give, q_acc = refs[:-1], refs[-1]
    top = tops[...]
    for o, cols in enumerate((col0, col1, col2, col3)):
        batch, hard = block_scores(scores, o)
        weights = jnp.exp(batch - top)
        if o == 0:
            weights = jnp.where(is_target(), 0.0, weights)
        both = block_weights(weights, jnp.exp(hard - top), asked[o : o + 1, :])
        term = lax.dot_general(both, cols[...], (((0,), (0,)), ((), ())), preferred_element_type=F32)
        if o == 0:
            q_acc[...] = term
        elif o < NB - 1:
            q_acc[...] += term
        else:
            total = (q_acc[...] + term).astype(BF16)
            keep[...] = total[0:256, :]
            for i, piece in enumerate(give):
                piece[...] = total[256 + i * 128 : 256 + (i + 1) * 128, :]


def join_kernel(stats, keep, *refs):
    came, (sent, logs) = refs[:-2], refs[-2:]
    zp = lax.axis_index("zp")
    z = lax.axis_index("zh") * 2 + zp
    absolute = []
    for l in range(4):
        tops = stats[:, l, :]
        top = jnp.max(tops, axis=0, keepdims=True)
        absolute.append(top + jnp.log(jnp.sum(stats[:, 4 + l, :] * jnp.exp(tops - top), axis=0, keepdims=True)))
    mine = stats[z]
    other = stats[z ^ 1]
    relative = [jnp.where(zp == 0, absolute[l], absolute[l ^ 2]) for l in range(4)]
    logs[...] = jnp.concatenate(relative, axis=1)
    rows = []
    for tops in (mine, other):
        for l in range(2):
            rows.append(jnp.exp(jnp.where(zp == 0, tops[l : l + 1, :], tops[l + 2 : l + 3, :]) - relative[l]))
    factors = jnp.concatenate(rows + [jnp.zeros((124, 128), F32)], axis=0).T
    for l in range(2):
        lines = slice(l * 128, (l + 1) * 128)
        other = jnp.concatenate([piece[...] for piece in came[l * 1 : (l + 1) * 1]], axis=0).astype(F32)
        total = keep[lines, :].astype(F32) * factors[:, l : l + 1] + other * factors[:, 2 + l : 3 + l]
        sent[l * 4 : (l + 1) * 4] = total.astype(BF16).reshape(4, 32, 512)


def column_grad_kernel(logs, scores, asked, queries, keep, give, at_target):
    log_total = logs[...]
    every = queries[...]
    for o in range(NB):
        batch, hard = block_scores(scores, o)
        weights = jnp.exp(batch - log_total)
        if o == 0:
            target = is_target()
            weights = jnp.where(target, weights - 1.0, weights)
            own = jnp.sum(jnp.where(target, weights, 0.0), axis=1, keepdims=True)
            at_target[...] = jnp.broadcast_to(own.astype(BF16).astype(F32), (32, 128))
        both = block_weights(weights, jnp.exp(hard - log_total), asked[o : o + 1, :])
        (give if o % 2 else keep)[o // 2] = jnp.dot(both, every, preferred_element_type=F32).astype(BF16)


def pair_kernel(keep, came, own, sent):
    own[...] = keep[0].astype(F32) + came[0].astype(F32)
    sent[...] = (keep[1].astype(F32) + came[1].astype(F32)).astype(BF16)


def column_kernel(own, came, passage_out, negative_out):
    passage_out[...] = (own[0:32, :] + came[0:32, :].astype(F32)).astype(BF16)
    negative_out[...] = (own[32:256, :] + came[32:256, :].astype(F32)).astype(BF16)


def query_kernel(came, at_target, passages, query_out):
    total = at_target[:, 0:1] * passages[...].astype(F32)
    for z in range(NH):
        total = total + came[z].astype(F32)
    query_out[...] = total.astype(BF16)


def swap(x, axis):
    return lax.ppermute(x, axis, [(0, 1), (1, 0)])


def exchange(x, axes):
    return lax.all_to_all(x, axes, split_axis=0, concat_axis=0, tiled=True)


def shards(queries, passages, negatives, hard_owner, hard_row):
    (sent,) = call(
        pack_kernel, [((NH, 144, 128), BF16)],
        queries, hard_owner.T, hard_row.T, hbm=3, limit=PACK_LIMIT,
        scratch=[
            pltpu.VMEM((32, 512), BF16), pltpu.VMEM((2, 7, 32), jnp.int32), pltpu.VMEM((2, 7, 128), jnp.int32),
            pltpu.SemaphoreType.DMA((3,)),
        ],
    )
    near = exchange(sent, "zh")
    far = swap(near, "zp")
    (col0,) = call(
        column_pack_kernel, [((256, 512), BF16)], passages, negatives, hbm=2,
        scratch=[pltpu.SemaphoreType.DMA((2,))],
    )
    col2 = swap(col0, "yh")
    col1 = swap(col0, "c")
    col3 = swap(col2, "c")
    parts, every, asked = call(
        score_kernel, [((8, 72, 128), F32), ((ROWS, 512), BF16), ((8, ROWS), jnp.int32)],
        near, far, col0, col1, col2, col3,
    )
    (summed,) = call(add_kernel, [((8, 72, 128), F32)], exchange(parts, ("yl", "x")))
    scores = exchange(summed, ("yl", "x"))
    stats, tops = call(stat_kernel, [((NZ, 8, 128), F32), ((1, ROWS), F32)], scores)
    stats = exchange(stats, ("zh", "zp"))
    q_keep, *q_give = call(
        share_kernel, [((256, 512), BF16)] + [((128, 512), BF16)] * 2,
        scores, tops, asked, col0, col1, col2, col3, scratch=[pltpu.VMEM((ROWS, 512), F32)],
    )
    q_pair, logs = call(
        join_kernel, [((NH, 32, 512), BF16), ((1, ROWS), F32)], stats, q_keep, *[swap(piece, "zp") for piece in q_give]
    )
    q_came = exchange(q_pair, "zh")
    keep, give, at_target = call(
        column_grad_kernel, [((2, 256, 512), BF16), ((2, 256, 512), BF16), ((32, 128), F32)],
        logs, scores, asked, every,
    )
    own, cross = call(pair_kernel, [((256, 512), F32), ((256, 512), BF16)], keep, swap(give, "c"))
    cross = swap(cross, "yh")
    passage_out, negative_out = call(column_kernel, [((32, 512), BF16), ((224, 512), BF16)], own, cross)
    (query_out,) = call(query_kernel, [((32, 512), BF16)], q_came, at_target, passages)
    return (query_out, passage_out, negative_out)


def solution(mesh):
    fine = Mesh(mesh.devices.reshape(2, NH, 2, 2, 2, 4), ("yh", "zh", "zp", "c", "yl", "x"))
    dp, mp = ("yh", "zh", "zp", "c"), ("yl", "x")
    return jax.shard_map(
        shards,
        mesh=fine,
        in_specs=(P(dp, mp), P(dp, mp), P(dp, mp), P(dp, None), P(dp, None)),
        out_specs=(P(dp, mp), P(dp, mp), P(dp, mp)),
        check_vma=False,
    )
```

```python
import math

import jax
import jax.numpy as jnp
from jax import lax
from jax.experimental import pallas as pl
from jax.experimental.pallas import tpu as pltpu
from jax.sharding import Mesh
from jax.sharding import PartitionSpec as P

BF16 = jnp.bfloat16
F32 = jnp.float32
NZ = 16
NH = 8
NB = 4
ROWS = 512
ABSENT = -1e30
VMEM_LIMIT = 48 * 1024 * 1024
PACK_LIMIT = 62 * 1024 * 1024


def call(kernel, out_shapes, *args, hbm=0, scratch=(), limit=VMEM_LIMIT):
    specs = [pl.BlockSpec(memory_space=pl.ANY)] * hbm
    specs += [pl.BlockSpec(memory_space=pltpu.VMEM)] * (len(args) - hbm)
    return pl.pallas_call(
        kernel,
        out_shape=[jax.ShapeDtypeStruct(shape, dtype) for shape, dtype in out_shapes],
        in_specs=specs,
        out_specs=[pl.BlockSpec(memory_space=pltpu.VMEM)] * len(out_shapes),
        scratch_shapes=list(scratch),
        compiler_params=pltpu.CompilerParams(vmem_limit_bytes=limit),
    )(*args)


def pack_kernel(queries, owners, rows, sent, mine, short, wide, sems):
    copies = [
        pltpu.make_async_copy(owners, short.at[0], sems.at[0]),
        pltpu.make_async_copy(rows, short.at[1], sems.at[1]),
        pltpu.make_async_copy(queries, mine, sems.at[2]),
    ]
    for copy in copies:
        copy.start()
    yh, zh, zp, c = (lax.axis_index(axis) for axis in ("yh", "zh", "zp", "c"))
    line = lax.broadcasted_iota(jnp.int32, (NH * 16, 128), 0)
    lane = lax.broadcasted_iota(jnp.int32, (NH * 16, 128), 1)
    block = line % 16
    z = (line // 16) * 2 + (zp ^ (block // 4))
    owner = ((yh ^ (block // 2 % 2)) * NZ + z) * 2 + (c ^ (block % 2))
    owner = jnp.where((block < 2 * NB) & (lane // 32 == zh % 4), owner, -2)
    copies[0].wait()
    copies[1].wait()
    for j in range(4):
        wide[:, :, j * 32 : (j + 1) * 32] = short[...]
    asked = jnp.full((NH * 16, 128), -1, jnp.int32)
    for k in range(short.shape[1]):
        asked = jnp.where(wide[0, k : k + 1, :] == owner, wide[1, k : k + 1, :], asked)
    asked = asked.astype(F32).astype(BF16)
    for to in range(NH):
        sent[to, 128:144, :] = asked[to * 16 : (to + 1) * 16, :]
    copies[2].wait()
    for to in range(NH):
        for l in range(4):
            sent[to, l * 32 : (l + 1) * 32, :] = mine[:, l * 128 : (l + 1) * 128]


def column_pack_kernel(passages, negatives, columns, sems):
    copies = [
        pltpu.make_async_copy(negatives, columns.at[32:256], sems.at[0]),
        pltpu.make_async_copy(passages, columns.at[0:32], sems.at[1]),
    ]
    for copy in copies:
        copy.start()
    for copy in copies:
        copy.wait()


def score_kernel(near, far, col0, col1, col2, col3, parts, queries, asked):
    scale = 3.0 / math.sqrt(4096)
    for s, came in enumerate((near, far)):
        for z in range(NH):
            for l in range(4):
                rows = slice((s * NH + z) * 32, (s * NH + z + 1) * 32)
                queries[rows, l * 128 : (l + 1) * 128] = came[z, l * 32 : (l + 1) * 32, :]
        for g in range(2):
            rows = came[4 * g, 128:144, :].astype(F32)
            for z in range(4 * g + 1, 4 * g + 4):
                rows = jnp.maximum(rows, came[z, 128:144, :].astype(F32))
            rows = rows[s * NB : (s + 1) * NB, :].astype(jnp.int32)
            asked[0:NB, (2 * s + g) * 128 : (2 * s + g + 1) * 128] = rows
    asked[NB:8, :] = jnp.full((8 - NB, ROWS), -1, jnp.int32)
    every = queries[...]
    place = lax.broadcasted_iota(jnp.int32, (224, ROWS), 0)
    for o, cols in enumerate((col0, col1, col2, col3)):
        part = lax.dot_general(cols[...], every, (((1,), (1,)), ((), ())), preferred_element_type=F32)
        want = asked[o : o + 1, :]
        hard = jnp.sum(jnp.where(place == want, part[32:256, :], 0.0), axis=0, keepdims=True) * scale
        hard = jnp.where(want >= 0, hard, ABSENT)
        h, a = o // 2, o % 2
        for l in range(4):
            lanes = slice(l * 128, (l + 1) * 128)
            parts[h * 4 + l, a * 32 : (a + 1) * 32, :] = part[0:32, lanes] * scale
            parts[h * 4 + l, 64 + a : 65 + a, :] = hard[:, lanes]
            if a == 1:
                parts[h * 4 + l, 66:72, :] = jnp.zeros((6, 128), F32)


def add_kernel(came, sent):
    total = came[0]
    for i in range(1, 8):
        total = total + came[i]
    for i in range(8):
        sent[i] = total


def stat_kernel(scores, sent, tops):
    zp = lax.axis_index("zp")
    pairs = []
    for l in range(4):
        batch = [scores[h * 4 + l, 0:64, :] for h in range(2)]
        hard = [scores[h * 4 + l, 64:66, :] for h in range(2)]
        top = jnp.maximum(
            jnp.max(jnp.maximum(batch[0], batch[1]), axis=0, keepdims=True),
            jnp.max(jnp.maximum(hard[0], hard[1]), axis=0, keepdims=True),
        )
        total = jnp.sum(jnp.exp(batch[0] - top) + jnp.exp(batch[1] - top), axis=0, keepdims=True)
        total = total + jnp.sum(jnp.exp(hard[0] - top) + jnp.exp(hard[1] - top), axis=0, keepdims=True)
        pairs.append((top, total))
    tops[...] = jnp.concatenate([top for top, _ in pairs], axis=1)
    for l in range(4):
        for k in range(2):
            row = jnp.where(zp == 0, pairs[l][k], pairs[l ^ 2][k])
            for to in range(NZ):
                sent[to, 4 * k + l : 4 * k + l + 1, :] = row


def block_scores(scores, o):
    h, a = o // 2, o % 2
    batch = jnp.concatenate([scores[h * 4 + l, a * 32 : (a + 1) * 32, :] for l in range(4)], axis=1)
    hard = jnp.concatenate([scores[h * 4 + l, 64 + a : 65 + a, :] for l in range(4)], axis=1)
    return batch, hard


def block_weights(batch, hard, want):
    line = lax.broadcasted_iota(jnp.int32, (224, ROWS), 0)
    hard = jnp.where(line == want, hard, 0.0)
    return jnp.concatenate([batch.astype(BF16), hard.astype(BF16)], axis=0)


def is_target():
    zh = lax.axis_index("zh")
    row = lax.broadcasted_iota(jnp.int32, (32, ROWS), 0)
    lane = lax.broadcasted_iota(jnp.int32, (32, ROWS), 1)
    return lane == zh * 32 + row


def share_kernel(scores, tops, asked, col0, col1, col2, col3, keep, *refs):
    give, q_acc = refs[:-1], refs[-1]
    top = tops[...]
    for o, cols in enumerate((col0, col1, col2, col3)):
        batch, hard = block_scores(scores, o)
        weights = jnp.exp(batch - top)
        if o == 0:
            weights = jnp.where(is_target(), 0.0, weights)
        both = block_weights(weights, jnp.exp(hard - top), asked[o : o + 1, :])
        term = lax.dot_general(both, cols[...], (((0,), (0,)), ((), ())), preferred_element_type=F32)
        if o == 0:
            q_acc[...] = term
        elif o < NB - 1:
            q_acc[...] += term
        else:
            total = (q_acc[...] + term).astype(BF16)
            keep[...] = total[0:256, :]
            for i, piece in enumerate(give):
                piece[...] = total[256 + i * 128 : 256 + (i + 1) * 128, :]


def column_grad_kernel(*refs):
    stats, scores, asked, queries, keep, give, at_target, logs = refs[2:]
    zp = lax.axis_index("zp")
    absolute = []
    for l in range(4):
        tops = stats[:, l, :]
        top = jnp.max(tops, axis=0, keepdims=True)
        absolute.append(top + jnp.log(jnp.sum(stats[:, 4 + l, :] * jnp.exp(tops - top), axis=0, keepdims=True)))
    log_total = jnp.concatenate([jnp.where(zp == 0, absolute[l], absolute[l ^ 2]) for l in range(4)], axis=1)
    logs[...] = log_total
    every = queries[...]
    for o in range(NB):
        batch, hard = block_scores(scores, o)
        weights = jnp.exp(batch - log_total)
        if o == 0:
            target = is_target()
            weights = jnp.where(target, weights - 1.0, weights)
            own = jnp.sum(jnp.where(target, weights, 0.0), axis=1, keepdims=True)
            at_target[...] = jnp.broadcast_to(own.astype(BF16).astype(F32), (32, 128))
        both = block_weights(weights, jnp.exp(hard - log_total), asked[o : o + 1, :])
        (give if o % 2 else keep)[o // 2] = jnp.dot(both, every, preferred_element_type=F32)


def join_kernel(stats, logs, keep, *refs):
    came, (sent,) = refs[:-1], refs[-1:]
    zp = lax.axis_index("zp")
    z = lax.axis_index("zh") * 2 + zp
    rows = []
    for tops in (stats[z], stats[z ^ 1]):
        for l in range(2):
            top = jnp.where(zp == 0, tops[l : l + 1, :], tops[l + 2 : l + 3, :])
            rows.append(jnp.exp(top - logs[:, l * 128 : (l + 1) * 128]))
    factors = jnp.concatenate(rows + [jnp.zeros((124, 128), F32)], axis=0).T
    for l in range(2):
        lines = slice(l * 128, (l + 1) * 128)
        total = keep[lines, :].astype(F32) * factors[:, l : l + 1]
        total = total + came[l][...].astype(F32) * factors[:, 2 + l : 3 + l]
        sent[l * 4 : (l + 1) * 4] = total.astype(BF16).reshape(4, 32, 512)


def pair_kernel(keep, came, own, sent):
    own[...] = keep[0] + came[0]
    sent[...] = (keep[1] + came[1]).astype(BF16)


def column_kernel(own, came, passage_out, negative_out):
    passage_out[...] = (own[0:32, :] + came[0:32, :].astype(F32)).astype(BF16)
    negative_out[...] = (own[32:256, :] + came[32:256, :].astype(F32)).astype(BF16)


def query_kernel(came, at_target, passages, query_out):
    total = at_target[:, 0:1] * passages[...].astype(F32)
    for z in range(NH):
        total = total + came[z].astype(F32)
    query_out[...] = total.astype(BF16)


def swap(x, axis):
    return lax.ppermute(x, axis, [(0, 1), (1, 0)])


def exchange(x, axes):
    return lax.all_to_all(x, axes, split_axis=0, concat_axis=0, tiled=True)


def shards(queries, passages, negatives, hard_owner, hard_row):
    (sent,) = call(
        pack_kernel, [((NH, 144, 128), BF16)],
        queries, hard_owner.T, hard_row.T, hbm=3, limit=PACK_LIMIT,
        scratch=[
            pltpu.VMEM((32, 512), BF16), pltpu.VMEM((2, 7, 32), jnp.int32), pltpu.VMEM((2, 7, 128), jnp.int32),
            pltpu.SemaphoreType.DMA((3,)),
        ],
    )
    near = exchange(sent, "zh")
    far = swap(near, "zp")
    (col0,) = call(
        column_pack_kernel, [((256, 512), BF16)], passages, negatives, hbm=2,
        scratch=[pltpu.SemaphoreType.DMA((2,))],
    )
    col2 = swap(col0, "yh")
    col1 = swap(col0, "c")
    col3 = swap(col2, "c")
    parts, every, asked = call(
        score_kernel, [((8, 72, 128), F32), ((ROWS, 512), BF16), ((8, ROWS), jnp.int32)],
        near, far, col0, col1, col2, col3,
    )
    (summed,) = call(add_kernel, [((8, 72, 128), F32)], exchange(parts, ("yl", "x")))
    scores = exchange(summed, ("yl", "x"))
    stats, tops = call(stat_kernel, [((NZ, 8, 128), F32), ((1, ROWS), F32)], scores)
    stats = exchange(stats, ("zh", "zp"))
    q_keep, *q_give = call(
        share_kernel, [((256, 512), BF16)] + [((128, 512), BF16)] * 2,
        scores, tops, asked, col0, col1, col2, col3, scratch=[pltpu.VMEM((ROWS, 512), F32)],
    )
    q_swapped = [swap(piece, "zp") for piece in q_give]
    keep, give, at_target, logs = call(
        column_grad_kernel,
        [((2, 256, 512), F32), ((2, 256, 512), F32), ((32, 128), F32), ((1, ROWS), F32)],
        *q_swapped, stats, scores, asked, every, hbm=2,
    )
    (q_pair,) = call(join_kernel, [((NH, 32, 512), BF16)], stats, logs, q_keep, *q_swapped)
    q_came = exchange(q_pair, "zh")
    own, cross = call(pair_kernel, [((256, 512), F32), ((256, 512), BF16)], keep, swap(give, "c"))
    cross = swap(cross, "yh")
    passage_out, negative_out = call(column_kernel, [((32, 512), BF16), ((224, 512), BF16)], own, cross)
    (query_out,) = call(query_kernel, [((32, 512), BF16)], q_came, at_target, passages)
    return (query_out, passage_out, negative_out)


def solution(mesh):
    fine = Mesh(mesh.devices.reshape(2, NH, 2, 2, 2, 4), ("yh", "zh", "zp", "c", "yl", "x"))
    dp, mp = ("yh", "zh", "zp", "c"), ("yl", "x")
    return jax.shard_map(
        shards,
        mesh=fine,
        in_specs=(P(dp, mp), P(dp, mp), P(dp, mp), P(dp, None), P(dp, None)),
        out_specs=(P(dp, mp), P(dp, mp), P(dp, mp)),
        check_vma=False,
    )
```

```python
import math

import jax
import jax.numpy as jnp
from jax import lax
from jax.experimental import pallas as pl
from jax.experimental.pallas import tpu as pltpu
from jax.sharding import Mesh
from jax.sharding import PartitionSpec as P

BF16 = jnp.bfloat16
F32 = jnp.float32
NZ = 16
NH = 8
NB = 4
ROWS = 512
ABSENT = -1e30
VMEM_LIMIT = 48 * 1024 * 1024
PACK_LIMIT = 62 * 1024 * 1024


def call(kernel, out_shapes, *args, hbm=0, scratch=(), limit=VMEM_LIMIT):
    specs = [pl.BlockSpec(memory_space=pl.ANY)] * hbm
    specs += [pl.BlockSpec(memory_space=pltpu.VMEM)] * (len(args) - hbm)
    return pl.pallas_call(
        kernel,
        out_shape=[jax.ShapeDtypeStruct(shape, dtype) for shape, dtype in out_shapes],
        in_specs=specs,
        out_specs=[pl.BlockSpec(memory_space=pltpu.VMEM)] * len(out_shapes),
        scratch_shapes=list(scratch),
        compiler_params=pltpu.CompilerParams(vmem_limit_bytes=limit),
    )(*args)


def pack_kernel(queries, owners, rows, sent, mine, short, wide, sems):
    copies = [
        pltpu.make_async_copy(owners, short.at[0], sems.at[0]),
        pltpu.make_async_copy(rows, short.at[1], sems.at[1]),
        pltpu.make_async_copy(queries, mine, sems.at[2]),
    ]
    for copy in copies:
        copy.start()
    yh, zh, zp, c = (lax.axis_index(axis) for axis in ("yh", "zh", "zp", "c"))
    line = lax.broadcasted_iota(jnp.int32, (NH * 16, 128), 0)
    lane = lax.broadcasted_iota(jnp.int32, (NH * 16, 128), 1)
    block = line % 16
    z = (line // 16) * 2 + (zp ^ (block // 4))
    owner = ((yh ^ (block // 2 % 2)) * NZ + z) * 2 + (c ^ (block % 2))
    owner = jnp.where((block < 2 * NB) & (lane // 32 == zh % 4), owner, -2)
    copies[0].wait()
    copies[1].wait()
    for j in range(4):
        wide[:, :, j * 32 : (j + 1) * 32] = short[...]
    asked = jnp.full((NH * 16, 128), -1, jnp.int32)
    for k in range(short.shape[1]):
        asked = jnp.where(wide[0, k : k + 1, :] == owner, wide[1, k : k + 1, :], asked)
    asked = asked.astype(F32).astype(BF16)
    for to in range(NH):
        sent[to, 128:144, :] = asked[to * 16 : (to + 1) * 16, :]
    copies[2].wait()
    for to in range(NH):
        for l in range(4):
            sent[to, l * 32 : (l + 1) * 32, :] = mine[:, l * 128 : (l + 1) * 128]


def column_pack_kernel(passages, negatives, columns, sems):
    copies = [
        pltpu.make_async_copy(negatives, columns.at[32:256], sems.at[0]),
        pltpu.make_async_copy(passages, columns.at[0:32], sems.at[1]),
    ]
    for copy in copies:
        copy.start()
    for copy in copies:
        copy.wait()


def score_kernel(near, far, col0, col1, col2, col3, parts, queries, asked):
    scale = 3.0 / math.sqrt(4096)
    for s, came in enumerate((near, far)):
        for z in range(NH):
            for l in range(4):
                rows = slice((s * NH + z) * 32, (s * NH + z + 1) * 32)
                queries[rows, l * 128 : (l + 1) * 128] = came[z, l * 32 : (l + 1) * 32, :]
        for g in range(2):
            rows = came[4 * g, 128:144, :].astype(F32)
            for z in range(4 * g + 1, 4 * g + 4):
                rows = jnp.maximum(rows, came[z, 128:144, :].astype(F32))
            rows = rows[s * NB : (s + 1) * NB, :].astype(jnp.int32)
            asked[0:NB, (2 * s + g) * 128 : (2 * s + g + 1) * 128] = rows
    asked[NB:8, :] = jnp.full((8 - NB, ROWS), -1, jnp.int32)
    every = queries[...]
    place = lax.broadcasted_iota(jnp.int32, (224, ROWS), 0)
    for o, cols in enumerate((col0, col1, col2, col3)):
        part = lax.dot_general(cols[...], every, (((1,), (1,)), ((), ())), preferred_element_type=F32)
        want = asked[o : o + 1, :]
        hard = jnp.sum(jnp.where(place == want, part[32:256, :], 0.0), axis=0, keepdims=True) * scale
        hard = jnp.where(want >= 0, hard, ABSENT)
        h, a = o // 2, o % 2
        for l in range(4):
            lanes = slice(l * 128, (l + 1) * 128)
            parts[h * 4 + l, a * 32 : (a + 1) * 32, :] = part[0:32, lanes] * scale
            parts[h * 4 + l, 64 + a : 65 + a, :] = hard[:, lanes]
            if a == 1:
                parts[h * 4 + l, 66:72, :] = jnp.zeros((6, 128), F32)


def add_kernel(came, sent):
    total = came[0]
    for i in range(1, 8):
        total = total + came[i]
    for i in range(8):
        sent[i] = total


def stat_kernel(scores, sent, tops):
    zp = lax.axis_index("zp")
    pairs = []
    for l in range(4):
        batch = [scores[h * 4 + l, 0:64, :] for h in range(2)]
        hard = [scores[h * 4 + l, 64:66, :] for h in range(2)]
        top = jnp.maximum(
            jnp.max(jnp.maximum(batch[0], batch[1]), axis=0, keepdims=True),
            jnp.max(jnp.maximum(hard[0], hard[1]), axis=0, keepdims=True),
        )
        total = jnp.sum(jnp.exp(batch[0] - top) + jnp.exp(batch[1] - top), axis=0, keepdims=True)
        total = total + jnp.sum(jnp.exp(hard[0] - top) + jnp.exp(hard[1] - top), axis=0, keepdims=True)
        pairs.append((top, total))
    tops[...] = jnp.concatenate([top for top, _ in pairs], axis=1)
    for l in range(4):
        for k in range(2):
            row = jnp.where(zp == 0, pairs[l][k], pairs[l ^ 2][k])
            for to in range(NZ):
                sent[to, 4 * k + l : 4 * k + l + 1, :] = row


def block_scores(scores, o):
    h, a = o // 2, o % 2
    batch = jnp.concatenate([scores[h * 4 + l, a * 32 : (a + 1) * 32, :] for l in range(4)], axis=1)
    hard = jnp.concatenate([scores[h * 4 + l, 64 + a : 65 + a, :] for l in range(4)], axis=1)
    return batch, hard


def block_weights(batch, hard, want):
    line = lax.broadcasted_iota(jnp.int32, (224, ROWS), 0)
    hard = jnp.where(line == want, hard, 0.0)
    return jnp.concatenate([batch.astype(BF16), hard.astype(BF16)], axis=0)


def is_target():
    zh = lax.axis_index("zh")
    row = lax.broadcasted_iota(jnp.int32, (32, ROWS), 0)
    lane = lax.broadcasted_iota(jnp.int32, (32, ROWS), 1)
    return lane == zh * 32 + row


def share_kernel(scores, tops, asked, col0, col1, col2, col3, keep, *refs):
    give, q_acc = refs[:-1], refs[-1]
    top = tops[...]
    for o, cols in enumerate((col0, col1, col2, col3)):
        batch, hard = block_scores(scores, o)
        weights = jnp.exp(batch - top)
        if o == 0:
            weights = jnp.where(is_target(), 0.0, weights)
        both = block_weights(weights, jnp.exp(hard - top), asked[o : o + 1, :])
        term = lax.dot_general(both, cols[...], (((0,), (0,)), ((), ())), preferred_element_type=F32)
        if o == 0:
            q_acc[...] = term
        elif o < NB - 1:
            q_acc[...] += term
        else:
            total = (q_acc[...] + term).astype(BF16)
            keep[...] = total[0:256, :]
            for i, piece in enumerate(give):
                piece[...] = total[256 + i * 128 : 256 + (i + 1) * 128, :]


def join_kernel(stats, keep, *refs):
    came, (sent, logs) = refs[:-2], refs[-2:]
    zp = lax.axis_index("zp")
    z = lax.axis_index("zh") * 2 + zp
    absolute = []
    for l in range(4):
        tops = stats[:, l, :]
        top = jnp.max(tops, axis=0, keepdims=True)
        absolute.append(top + jnp.log(jnp.sum(stats[:, 4 + l, :] * jnp.exp(tops - top), axis=0, keepdims=True)))
    mine = stats[z]
    other = stats[z ^ 1]
    relative = [jnp.where(zp == 0, absolute[l], absolute[l ^ 2]) for l in range(4)]
    logs[...] = jnp.concatenate(relative, axis=1)
    rows = []
    for tops in (mine, other):
        for l in range(2):
            rows.append(jnp.exp(jnp.where(zp == 0, tops[l : l + 1, :], tops[l + 2 : l + 3, :]) - relative[l]))
    factors = jnp.concatenate(rows + [jnp.zeros((124, 128), F32)], axis=0).T
    for l in range(2):
        lines = slice(l * 128, (l + 1) * 128)
        other = jnp.concatenate([piece[...] for piece in came[l * 1 : (l + 1) * 1]], axis=0).astype(F32)
        total = keep[lines, :].astype(F32) * factors[:, l : l + 1] + other * factors[:, 2 + l : 3 + l]
        sent[l * 4 : (l + 1) * 4] = total.astype(BF16).reshape(4, 32, 512)


def column_grad_kernel(logs, scores, asked, queries, own, core, other, cross, at_target):
    log_total = logs[...]
    every = queries[...]
    for o in range(NB):
        batch, hard = block_scores(scores, o)
        weights = jnp.exp(batch - log_total)
        if o == 0:
            target = is_target()
            weights = jnp.where(target, weights - 1.0, weights)
            mine = jnp.sum(jnp.where(target, weights, 0.0), axis=1, keepdims=True)
            at_target[...] = jnp.broadcast_to(mine.astype(BF16).astype(F32), (32, 128))
        both = block_weights(weights, jnp.exp(hard - log_total), asked[o : o + 1, :])
        out = (own, core, other, cross)[o]
        out[...] = jnp.dot(both, every, preferred_element_type=F32).astype(out.dtype)


def column_kernel(own, cross, other, core, passage_out, negative_out):
    for out, rows in ((passage_out, slice(0, 32)), (negative_out, slice(32, 256))):
        total = own[rows, :] + core[rows, :].astype(F32)
        out[...] = (total + other[rows, :].astype(F32) + cross[rows, :].astype(F32)).astype(BF16)


def query_kernel(came, at_target, passages, query_out):
    total = at_target[:, 0:1] * passages[...].astype(F32)
    for z in range(NH):
        total = total + came[z].astype(F32)
    query_out[...] = total.astype(BF16)


def swap(x, axis):
    return lax.ppermute(x, axis, [(0, 1), (1, 0)])


def exchange(x, axes):
    return lax.all_to_all(x, axes, split_axis=0, concat_axis=0, tiled=True)


def shards(queries, passages, negatives, hard_owner, hard_row):
    (sent,) = call(
        pack_kernel, [((NH, 144, 128), BF16)],
        queries, hard_owner.T, hard_row.T, hbm=3, limit=PACK_LIMIT,
        scratch=[
            pltpu.VMEM((32, 512), BF16), pltpu.VMEM((2, 7, 32), jnp.int32), pltpu.VMEM((2, 7, 128), jnp.int32),
            pltpu.SemaphoreType.DMA((3,)),
        ],
    )
    near = exchange(sent, "zh")
    far = swap(near, "zp")
    (col0,) = call(
        column_pack_kernel, [((256, 512), BF16)], passages, negatives, hbm=2,
        scratch=[pltpu.SemaphoreType.DMA((2,))],
    )
    col2 = swap(col0, "yh")
    col1 = swap(col0, "c")
    col3 = swap(col2, "c")
    parts, every, asked = call(
        score_kernel, [((8, 72, 128), F32), ((ROWS, 512), BF16), ((8, ROWS), jnp.int32)],
        near, far, col0, col1, col2, col3,
    )
    (summed,) = call(add_kernel, [((8, 72, 128), F32)], exchange(parts, ("yl", "x")))
    scores = exchange(summed, ("yl", "x"))
    stats, tops = call(stat_kernel, [((NZ, 8, 128), F32), ((1, ROWS), F32)], scores)
    stats = exchange(stats, ("zh", "zp"))
    q_keep, *q_give = call(
        share_kernel, [((256, 512), BF16)] + [((128, 512), BF16)] * 2,
        scores, tops, asked, col0, col1, col2, col3, scratch=[pltpu.VMEM((ROWS, 512), F32)],
    )
    q_pair, logs = call(
        join_kernel, [((NH, 32, 512), BF16), ((1, ROWS), F32)], stats, q_keep, *[swap(piece, "zp") for piece in q_give]
    )
    q_came = exchange(q_pair, "zh")
    own, core, other, cross, at_target = call(
        column_grad_kernel, [((256, 512), F32)] + [((256, 512), BF16)] * 3 + [((32, 128), F32)],
        logs, scores, asked, every,
    )
    passage_out, negative_out = call(
        column_kernel, [((32, 512), BF16), ((224, 512), BF16)],
        own, lax.ppermute(cross, ("yh", "c"), [(0, 3), (1, 2), (2, 1), (3, 0)]), swap(other, "yh"), swap(core, "c"),
    )
    (query_out,) = call(query_kernel, [((32, 512), BF16)], q_came, at_target, passages)
    return (query_out, passage_out, negative_out)


def solution(mesh):
    fine = Mesh(mesh.devices.reshape(2, NH, 2, 2, 2, 4), ("yh", "zh", "zp", "c", "yl", "x"))
    dp, mp = ("yh", "zh", "zp", "c"), ("yl", "x")
    return jax.shard_map(
        shards,
        mesh=fine,
        in_specs=(P(dp, mp), P(dp, mp), P(dp, mp), P(dp, None), P(dp, None)),
        out_specs=(P(dp, mp), P(dp, mp), P(dp, mp)),
        check_vma=False,
    )
```

```python
import math

import jax
import jax.numpy as jnp
from jax import lax
from jax.experimental import pallas as pl
from jax.experimental.pallas import tpu as pltpu
from jax.sharding import Mesh
from jax.sharding import PartitionSpec as P

BF16 = jnp.bfloat16
F32 = jnp.float32
NZ = 16
NH = 8
NB = 4
ROWS = 512
ABSENT = -1e30
VMEM_LIMIT = 48 * 1024 * 1024
PACK_LIMIT = 62 * 1024 * 1024


def call(kernel, out_shapes, *args, hbm=0, scratch=(), limit=VMEM_LIMIT):
    specs = [pl.BlockSpec(memory_space=pl.ANY)] * hbm
    specs += [pl.BlockSpec(memory_space=pltpu.VMEM)] * (len(args) - hbm)
    return pl.pallas_call(
        kernel,
        out_shape=[jax.ShapeDtypeStruct(shape, dtype) for shape, dtype in out_shapes],
        in_specs=specs,
        out_specs=[pl.BlockSpec(memory_space=pltpu.VMEM)] * len(out_shapes),
        scratch_shapes=list(scratch),
        compiler_params=pltpu.CompilerParams(vmem_limit_bytes=limit),
    )(*args)


def pack_kernel(queries, owners, rows, sent, mine, short, wide, sems):
    copies = [
        pltpu.make_async_copy(owners, short.at[0], sems.at[0]),
        pltpu.make_async_copy(rows, short.at[1], sems.at[1]),
        pltpu.make_async_copy(queries, mine, sems.at[2]),
    ]
    for copy in copies:
        copy.start()
    yh, zh, zp, c = (lax.axis_index(axis) for axis in ("yh", "zh", "zp", "c"))
    line = lax.broadcasted_iota(jnp.int32, (NH * 16, 128), 0)
    lane = lax.broadcasted_iota(jnp.int32, (NH * 16, 128), 1)
    block = line % 16
    z = (line // 16) * 2 + (zp ^ (block // 4))
    owner = ((yh ^ (block // 2 % 2)) * NZ + z) * 2 + (c ^ (block % 2))
    owner = jnp.where((block < 2 * NB) & (lane // 32 == zh % 4), owner, -2)
    copies[0].wait()
    copies[1].wait()
    for j in range(4):
        wide[:, :, j * 32 : (j + 1) * 32] = short[...]
    asked = jnp.full((NH * 16, 128), -1, jnp.int32)
    for k in range(short.shape[1]):
        asked = jnp.where(wide[0, k : k + 1, :] == owner, wide[1, k : k + 1, :], asked)
    asked = asked.astype(F32).astype(BF16)
    for to in range(NH):
        sent[to, 128:144, :] = asked[to * 16 : (to + 1) * 16, :]
    copies[2].wait()
    for to in range(NH):
        for l in range(4):
            sent[to, l * 32 : (l + 1) * 32, :] = mine[:, l * 128 : (l + 1) * 128]


def column_pack_kernel(passages, negatives, columns, sems):
    copies = [
        pltpu.make_async_copy(negatives, columns.at[32:256], sems.at[0]),
        pltpu.make_async_copy(passages, columns.at[0:32], sems.at[1]),
    ]
    for copy in copies:
        copy.start()
    for copy in copies:
        copy.wait()


def score_kernel(near, far, col0, col1, col2, col3, parts, queries, asked):
    scale = 3.0 / math.sqrt(4096)
    for s, came in enumerate((near, far)):
        for z in range(NH):
            for l in range(4):
                rows = slice((s * NH + z) * 32, (s * NH + z + 1) * 32)
                queries[rows, l * 128 : (l + 1) * 128] = came[z, l * 32 : (l + 1) * 32, :]
        for g in range(2):
            rows = came[4 * g, 128:144, :].astype(F32)
            for z in range(4 * g + 1, 4 * g + 4):
                rows = jnp.maximum(rows, came[z, 128:144, :].astype(F32))
            rows = rows[s * NB : (s + 1) * NB, :].astype(jnp.int32)
            asked[0:NB, (2 * s + g) * 128 : (2 * s + g + 1) * 128] = rows
    asked[NB:8, :] = jnp.full((8 - NB, ROWS), -1, jnp.int32)
    every = queries[...]
    place = lax.broadcasted_iota(jnp.int32, (224, ROWS), 0)
    for o, cols in enumerate((col0, col1, col2, col3)):
        part = lax.dot_general(cols[...], every, (((1,), (1,)), ((), ())), preferred_element_type=F32)
        want = asked[o : o + 1, :]
        hard = jnp.sum(jnp.where(place == want, part[32:256, :], 0.0), axis=0, keepdims=True) * scale
        hard = jnp.where(want >= 0, hard, ABSENT)
        h, a = o // 2, o % 2
        for l in range(4):
            lanes = slice(l * 128, (l + 1) * 128)
            parts[h * 4 + l, a * 32 : (a + 1) * 32, :] = part[0:32, lanes] * scale
            parts[h * 4 + l, 64 + a : 65 + a, :] = hard[:, lanes]
            if a == 1:
                parts[h * 4 + l, 66:72, :] = jnp.zeros((6, 128), F32)


def add_kernel(came, sent):
    total = came[0]
    for i in range(1, 8):
        total = total + came[i]
    for i in range(8):
        sent[i] = total


def stat_kernel(scores, sent, tops):
    zp = lax.axis_index("zp")
    pairs = []
    for l in range(4):
        batch = [scores[h * 4 + l, 0:64, :] for h in range(2)]
        hard = [scores[h * 4 + l, 64:66, :] for h in range(2)]
        top = jnp.maximum(
            jnp.max(jnp.maximum(batch[0], batch[1]), axis=0, keepdims=True),
            jnp.max(jnp.maximum(hard[0], hard[1]), axis=0, keepdims=True),
        )
        total = jnp.sum(jnp.exp(batch[0] - top) + jnp.exp(batch[1] - top), axis=0, keepdims=True)
        total = total + jnp.sum(jnp.exp(hard[0] - top) + jnp.exp(hard[1] - top), axis=0, keepdims=True)
        pairs.append((top, total))
    tops[...] = jnp.concatenate([top for top, _ in pairs], axis=1)
    for l in range(4):
        for k in range(2):
            row = jnp.where(zp == 0, pairs[l][k], pairs[l ^ 2][k])
            for to in range(NZ):
                sent[to, 4 * k + l : 4 * k + l + 1, :] = row


def block_scores(scores, o):
    h, a = o // 2, o % 2
    batch = jnp.concatenate([scores[h * 4 + l, a * 32 : (a + 1) * 32, :] for l in range(4)], axis=1)
    hard = jnp.concatenate([scores[h * 4 + l, 64 + a : 65 + a, :] for l in range(4)], axis=1)
    return batch, hard


def block_weights(batch, hard, want):
    line = lax.broadcasted_iota(jnp.int32, (224, ROWS), 0)
    hard = jnp.where(line == want, hard, 0.0)
    return jnp.concatenate([batch.astype(BF16), hard.astype(BF16)], axis=0)


def is_target():
    zh = lax.axis_index("zh")
    row = lax.broadcasted_iota(jnp.int32, (32, ROWS), 0)
    lane = lax.broadcasted_iota(jnp.int32, (32, ROWS), 1)
    return lane == zh * 32 + row


def share_kernel(scores, tops, asked, col0, col1, col2, col3, keep, *refs):
    give, q_acc = refs[:-1], refs[-1]
    top = tops[...]
    for o, cols in enumerate((col0, col1, col2, col3)):
        batch, hard = block_scores(scores, o)
        weights = jnp.exp(batch - top)
        if o == 0:
            weights = jnp.where(is_target(), 0.0, weights)
        both = block_weights(weights, jnp.exp(hard - top), asked[o : o + 1, :])
        term = lax.dot_general(both, cols[...], (((0,), (0,)), ((), ())), preferred_element_type=F32)
        if o == 0:
            q_acc[...] = term
        elif o < NB - 1:
            q_acc[...] += term
        else:
            total = (q_acc[...] + term).astype(BF16)
            keep[...] = total[0:256, :]
            for i, piece in enumerate(give):
                piece[...] = total[256 + i * 128 : 256 + (i + 1) * 128, :]


def join_kernel(stats, keep, *refs):
    came, (sent, logs) = refs[:-2], refs[-2:]
    zp = lax.axis_index("zp")
    z = lax.axis_index("zh") * 2 + zp
    absolute = []
    for l in range(4):
        tops = stats[:, l, :]
        top = jnp.max(tops, axis=0, keepdims=True)
        absolute.append(top + jnp.log(jnp.sum(stats[:, 4 + l, :] * jnp.exp(tops - top), axis=0, keepdims=True)))
    mine = stats[z]
    other = stats[z ^ 1]
    relative = [jnp.where(zp == 0, absolute[l], absolute[l ^ 2]) for l in range(4)]
    logs[...] = jnp.concatenate(relative, axis=1)
    rows = []
    for tops in (mine, other):
        for l in range(2):
            rows.append(jnp.exp(jnp.where(zp == 0, tops[l : l + 1, :], tops[l + 2 : l + 3, :]) - relative[l]))
    factors = jnp.concatenate(rows + [jnp.zeros((124, 128), F32)], axis=0).T
    for l in range(2):
        lines = slice(l * 128, (l + 1) * 128)
        other = jnp.concatenate([piece[...] for piece in came[l * 1 : (l + 1) * 1]], axis=0).astype(F32)
        total = keep[lines, :].astype(F32) * factors[:, l : l + 1] + other * factors[:, 2 + l : 3 + l]
        sent[l * 4 : (l + 1) * 4] = total.astype(BF16).reshape(4, 32, 512)


def column_grad_kernel(logs, scores, asked, queries, keep, give, at_target):
    log_total = logs[...]
    every = queries[...]
    for o in range(NB):
        batch, hard = block_scores(scores, o)
        weights = jnp.exp(batch - log_total)
        if o == 0:
            target = is_target()
            weights = jnp.where(target, weights - 1.0, weights)
            own = jnp.sum(jnp.where(target, weights, 0.0), axis=1, keepdims=True)
            at_target[...] = jnp.broadcast_to(own.astype(BF16).astype(F32), (32, 128))
        both = block_weights(weights, jnp.exp(hard - log_total), asked[o : o + 1, :])
        (give if o % 2 else keep)[o // 2] = jnp.dot(both, every, preferred_element_type=F32).astype(BF16)


def pair_kernel(keep, came, own, sent):
    own[...] = keep[0].astype(F32) + came[0].astype(F32)
    sent[...] = (keep[1].astype(F32) + came[1].astype(F32)).astype(BF16)


def column_kernel(own, came, passage_out, negative_out):
    passage_out[...] = (own[0:32, :] + came[0:32, :].astype(F32)).astype(BF16)
    negative_out[...] = (own[32:256, :] + came[32:256, :].astype(F32)).astype(BF16)


def query_kernel(came, at_target, passages, query_out):
    total = at_target[:, 0:1] * passages[...].astype(F32)
    for z in range(NH):
        total = total + came[z].astype(F32)
    query_out[...] = total.astype(BF16)


def after(x, *others):
    return pl.pallas_call(
        lambda *refs: None,
        out_shape=jax.ShapeDtypeStruct(x.shape, x.dtype),
        in_specs=[pl.BlockSpec(memory_space=pltpu.VMEM)] * (1 + len(others)),
        out_specs=pl.BlockSpec(memory_space=pltpu.VMEM),
        input_output_aliases={0: 0},
        compiler_params=pltpu.CompilerParams(vmem_limit_bytes=VMEM_LIMIT),
    )(x, *others)


def swap(x, axis):
    return lax.ppermute(x, axis, [(0, 1), (1, 0)])


def exchange(x, axes):
    return lax.all_to_all(x, axes, split_axis=0, concat_axis=0, tiled=True)


def shards(queries, passages, negatives, hard_owner, hard_row):
    (sent,) = call(
        pack_kernel, [((NH, 144, 128), BF16)],
        queries, hard_owner.T, hard_row.T, hbm=3, limit=PACK_LIMIT,
        scratch=[
            pltpu.VMEM((32, 512), BF16), pltpu.VMEM((2, 7, 32), jnp.int32), pltpu.VMEM((2, 7, 128), jnp.int32),
            pltpu.SemaphoreType.DMA((3,)),
        ],
    )
    near = exchange(sent, "zh")
    (col0,) = call(
        column_pack_kernel, [((256, 512), BF16)], passages, negatives, hbm=2,
        scratch=[pltpu.SemaphoreType.DMA((2,))],
    )
    col2 = swap(col0, "yh")
    col1 = swap(col0, "c")
    col3 = swap(col2, "c")
    near = after(near, col1, col3)
    far = swap(near, "zp")
    parts, every, asked = call(
        score_kernel, [((8, 72, 128), F32), ((ROWS, 512), BF16), ((8, ROWS), jnp.int32)],
        near, far, col0, col1, col2, col3,
    )
    (summed,) = call(add_kernel, [((8, 72, 128), F32)], exchange(parts, ("yl", "x")))
    scores = exchange(summed, ("yl", "x"))
    stats, tops = call(stat_kernel, [((NZ, 8, 128), F32), ((1, ROWS), F32)], scores)
    stats = exchange(stats, ("zh", "zp"))
    q_keep, *q_give = call(
        share_kernel, [((256, 512), BF16)] + [((128, 512), BF16)] * 2,
        scores, tops, asked, col0, col1, col2, col3, scratch=[pltpu.VMEM((ROWS, 512), F32)],
    )
    q_pair, logs = call(
        join_kernel, [((NH, 32, 512), BF16), ((1, ROWS), F32)], stats, q_keep, *[swap(piece, "zp") for piece in q_give]
    )
    q_came = exchange(q_pair, "zh")
    keep, give, at_target = call(
        column_grad_kernel, [((2, 256, 512), BF16), ((2, 256, 512), BF16), ((32, 128), F32)],
        logs, scores, asked, every,
    )
    own, cross = call(pair_kernel, [((256, 512), F32), ((256, 512), BF16)], keep, swap(give, "c"))
    cross = swap(cross, "yh")
    passage_out, negative_out = call(column_kernel, [((32, 512), BF16), ((224, 512), BF16)], own, cross)
    (query_out,) = call(query_kernel, [((32, 512), BF16)], q_came, at_target, passages)
    return (query_out, passage_out, negative_out)


def solution(mesh):
    fine = Mesh(mesh.devices.reshape(2, NH, 2, 2, 2, 4), ("yh", "zh", "zp", "c", "yl", "x"))
    dp, mp = ("yh", "zh", "zp", "c"), ("yl", "x")
    return jax.shard_map(
        shards,
        mesh=fine,
        in_specs=(P(dp, mp), P(dp, mp), P(dp, mp), P(dp, None), P(dp, None)),
        out_specs=(P(dp, mp), P(dp, mp), P(dp, mp)),
        check_vma=False,
    )
```

```python
import math

import jax
import jax.numpy as jnp
from jax import lax
from jax.experimental import pallas as pl
from jax.experimental.pallas import tpu as pltpu
from jax.sharding import Mesh
from jax.sharding import PartitionSpec as P

BF16 = jnp.bfloat16
F32 = jnp.float32
NZ = 16
NH = 8
NB = 8
ROWS = 256
ABSENT = -1e30
VMEM_LIMIT = 48 * 1024 * 1024
PACK_LIMIT = 62 * 1024 * 1024
HOLD_FLOPS = 1153000000


def call(kernel, out_shapes, *args, hbm=0, scratch=(), limit=VMEM_LIMIT):
    specs = [pl.BlockSpec(memory_space=pl.ANY)] * hbm
    specs += [pl.BlockSpec(memory_space=pltpu.VMEM)] * (len(args) - hbm)
    return pl.pallas_call(
        kernel,
        out_shape=[jax.ShapeDtypeStruct(shape, dtype) for shape, dtype in out_shapes],
        in_specs=specs,
        out_specs=[pl.BlockSpec(memory_space=pltpu.VMEM)] * len(out_shapes),
        scratch_shapes=list(scratch),
        compiler_params=pltpu.CompilerParams(vmem_limit_bytes=limit),
    )(*args)


def pack_kernel(queries, owners, rows, sent, mine, short, wide, sems):
    copies = [
        pltpu.make_async_copy(owners, short.at[0], sems.at[0]),
        pltpu.make_async_copy(rows, short.at[1], sems.at[1]),
        pltpu.make_async_copy(queries, mine, sems.at[2]),
    ]
    for copy in copies:
        copy.start()
    yh, zh, zp, c = (lax.axis_index(axis) for axis in ("yh", "zh", "zp", "c"))
    line = lax.broadcasted_iota(jnp.int32, (NH * 16, 128), 0)
    lane = lax.broadcasted_iota(jnp.int32, (NH * 16, 128), 1)
    block = line % 16
    z = (line // 16) * 2 + (zp ^ (block // 4))
    owner = ((yh ^ (block // 2 % 2)) * NZ + z) * 2 + (c ^ (block % 2))
    owner = jnp.where((block < NB) & (lane // 32 == zh % 4), owner, -2)
    copies[0].wait()
    copies[1].wait()
    for j in range(4):
        wide[:, :, j * 32 : (j + 1) * 32] = short[...]
    asked = jnp.full((NH * 16, 128), -1, jnp.int32)
    for k in range(short.shape[1]):
        asked = jnp.where(wide[0, k : k + 1, :] == owner, wide[1, k : k + 1, :], asked)
    asked = asked.astype(F32).astype(BF16)
    for to in range(NH):
        sent[to, 128:144, :] = asked[to * 16 : (to + 1) * 16, :]
    copies[2].wait()
    for to in range(NH):
        for l in range(4):
            sent[to, l * 32 : (l + 1) * 32, :] = mine[:, l * 128 : (l + 1) * 128]


def column_pack_kernel(passages, negatives, columns, sems):
    copies = [
        pltpu.make_async_copy(negatives, columns.at[32:256], sems.at[0]),
        pltpu.make_async_copy(passages, columns.at[0:32], sems.at[1]),
    ]
    for copy in copies:
        copy.start()
    for copy in copies:
        copy.wait()


def unpack(came, lines, queries, asked):
    for z in range(NH):
        for l in range(4):
            queries[z * 32 : (z + 1) * 32, l * 128 : (l + 1) * 128] = came[z, l * 32 : (l + 1) * 32, :]
    for g in range(2):
        rows = came[4 * g, 128:144, :].astype(F32)
        for z in range(4 * g + 1, 4 * g + 4):
            rows = jnp.maximum(rows, came[z, 128:144, :].astype(F32))
        asked[:, g * 128 : (g + 1) * 128] = rows[lines, :].astype(jnp.int32)


def stack_kernel(first, second, both):
    both[0:256, :] = first[...]
    both[256:512, :] = second[...]


def score_kernel(near, *refs):
    columns, (parts, queries, asked) = refs[:4], refs[4:]
    scale = 3.0 / math.sqrt(4096)
    unpack(near, slice(0, NB), queries, asked)
    every = queries[...]
    place = lax.broadcasted_iota(jnp.int32, (224, ROWS), 0)
    for o in range(NB):
        cols = columns[o % 4][o // 4 * 256 : (o // 4 + 1) * 256, :]
        part = lax.dot_general(cols, every, (((1,), (1,)), ((), ())), preferred_element_type=F32)
        want = asked[o : o + 1, :]
        hard = jnp.sum(jnp.where(place == want, part[32:256, :], 0.0), axis=0, keepdims=True) * scale
        hard = jnp.where(want >= 0, hard, ABSENT)
        h, a = o // 2, o % 2
        for l in range(2):
            lanes = slice(l * 128, (l + 1) * 128)
            parts[h * 2 + l, a * 32 : (a + 1) * 32, :] = part[0:32, lanes] * scale
            parts[h * 2 + l, 64 + a : 65 + a, :] = hard[:, lanes]
            if a == 1:
                parts[h * 2 + l, 66:72, :] = jnp.zeros((6, 128), F32)


def add_kernel(came, sent):
    total = came[0]
    for i in range(1, 8):
        total = total + came[i]
    for i in range(8):
        sent[i] = total


def stat_kernel(scores, sent, cross):
    cross[...] = scores[4:8]
    for l in range(2):
        batch = [scores[h * 2 + l, 0:64, :] for h in range(4)]
        hard = [scores[h * 2 + l, 64:66, :] for h in range(4)]
        top = jnp.maximum(
            jnp.max(jnp.maximum(jnp.maximum(batch[0], batch[1]), jnp.maximum(batch[2], batch[3])), axis=0, keepdims=True),
            jnp.max(jnp.maximum(jnp.maximum(hard[0], hard[1]), jnp.maximum(hard[2], hard[3])), axis=0, keepdims=True),
        )
        total = jnp.sum(sum(jnp.exp(b - top) for b in batch), axis=0, keepdims=True)
        total = total + jnp.sum(sum(jnp.exp(h - top) for h in hard), axis=0, keepdims=True)
        for to in range(NZ):
            sent[to, l : l + 1, :] = top
            sent[to, 2 + l : 3 + l, :] = total
    for to in range(NZ):
        sent[to, 4:8, :] = jnp.zeros((4, 128), F32)


def row_logs(stats, zp):
    logs = []
    for l in range(2):
        tops = jnp.where(zp == 0, stats[:, 0, l, :], stats[:, 1, l, :])
        totals = jnp.where(zp == 0, stats[:, 0, 2 + l, :], stats[:, 1, 2 + l, :])
        top = jnp.max(tops, axis=0, keepdims=True)
        logs.append(top + jnp.log(jnp.sum(totals * jnp.exp(tops - top), axis=0, keepdims=True)))
    return jnp.concatenate(logs, axis=1)


def block_weights(scores, o, logs, want, targets):
    h, a = o // 2, o % 2
    batch = jnp.concatenate([scores[h * 2 + l, a * 32 : (a + 1) * 32, :] for l in range(2)], axis=1)
    hard = jnp.concatenate([scores[h * 2 + l, 64 + a : 65 + a, :] for l in range(2)], axis=1)
    weights = jnp.exp(batch - logs)
    if targets and o == 0:
        row = lax.broadcasted_iota(jnp.int32, (32, ROWS), 0)
        lane = lax.broadcasted_iota(jnp.int32, (32, ROWS), 1)
        weights = weights - (lane == lax.axis_index("zh") * 32 + row).astype(F32)
    line = lax.broadcasted_iota(jnp.int32, (224, ROWS), 0)
    hard = jnp.where(line == want, jnp.exp(hard - logs), 0.0)
    return jnp.concatenate([weights.astype(BF16), hard.astype(BF16)], axis=0)


def share_kernel(stats, scores, asked, *refs):
    columns, (sent, logs, total) = refs[:4], refs[4:]
    zp = lax.axis_index("zp")
    near = row_logs(stats, zp)
    logs[0:1, :] = near
    logs[1:2, :] = row_logs(stats, 1 - zp)
    for o in range(NB):
        weights = block_weights(scores, o, near, asked[o : o + 1, :], True)
        cols = columns[o % 4][o // 4 * 256 : (o // 4 + 1) * 256, :]
        term = lax.dot_general(weights, cols, (((0,), (0,)), ((), ())), preferred_element_type=F32)
        if o == 0:
            total[...] = term
        elif o < NB - 1:
            total[...] += term
        else:
            sent[...] = (total[...] + term).astype(BF16).reshape(NH, 32, 512)


def column_grad_kernel(logs, scores, asked, queries, far_scores, far, keep, give, far_queries, far_asked):
    unpack(far, slice(4, 8), far_queries, far_asked)
    near_queries, other_queries = queries[...], far_queries[...]
    for o in range(4):
        weights = block_weights(scores, o, logs[0:1, :], asked[o : o + 1, :], True)
        grad = jnp.dot(weights, near_queries, preferred_element_type=F32)
        weights = block_weights(far_scores, o, logs[1:2, :], far_asked[o : o + 1, :], False)
        grad = grad + jnp.dot(weights, other_queries, preferred_element_type=F32)
        (give if o % 2 else keep)[o // 2] = grad.astype(BF16)


def pair_kernel(keep, came, own, sent):
    own[...] = keep[0].astype(F32) + came[0].astype(F32)
    sent[...] = (keep[1].astype(F32) + came[1].astype(F32)).astype(BF16)


def column_kernel(own, came, passage_out, negative_out):
    passage_out[...] = (own[0:32, :] + came[0:32, :].astype(F32)).astype(BF16)
    negative_out[...] = (own[32:256, :] + came[32:256, :].astype(F32)).astype(BF16)


def query_kernel(came, query_out):
    total = came[0].astype(F32)
    for z in range(1, NH):
        total = total + came[z].astype(F32)
    query_out[...] = total.astype(BF16)


def hold(x):
    return pl.pallas_call(
        lambda *refs: None,
        out_shape=jax.ShapeDtypeStruct(x.shape, x.dtype),
        in_specs=[pl.BlockSpec(memory_space=pltpu.VMEM)],
        out_specs=pl.BlockSpec(memory_space=pltpu.VMEM),
        input_output_aliases={0: 0},
        cost_estimate=pl.CostEstimate(flops=HOLD_FLOPS, bytes_accessed=0, transcendentals=0),
        compiler_params=pltpu.CompilerParams(vmem_limit_bytes=VMEM_LIMIT),
    )(x)


def swap(x, axis):
    return lax.ppermute(x, axis, [(0, 1), (1, 0)])


def exchange(x, axes):
    return lax.all_to_all(x, axes, split_axis=0, concat_axis=0, tiled=True)


def shards(queries, passages, negatives, hard_owner, hard_row):
    (sent,) = call(
        pack_kernel, [((NH, 144, 128), BF16)],
        queries, hard_owner.T, hard_row.T, hbm=3, limit=PACK_LIMIT,
        scratch=[
            pltpu.VMEM((32, 512), BF16), pltpu.VMEM((2, 7, 32), jnp.int32), pltpu.VMEM((2, 7, 128), jnp.int32),
            pltpu.SemaphoreType.DMA((3,)),
        ],
    )
    (col0,) = call(
        column_pack_kernel, [((256, 512), BF16)], passages, negatives, hbm=2,
        scratch=[pltpu.SemaphoreType.DMA((2,))],
    )
    (pair,) = call(stack_kernel, [((512, 512), BF16)], col0, swap(col0, "zp"))
    near = hold(exchange(sent, "zh"))
    other = swap(pair, "yh")
    columns = (pair, swap(pair, "c"), other, swap(other, "c"))
    parts, queries, asked = call(
        score_kernel, [((8, 72, 128), F32), ((ROWS, 512), BF16), ((NB, ROWS), jnp.int32)], near, *columns
    )
    far = swap(near, "zp")
    (summed,) = call(add_kernel, [((8, 72, 128), F32)], exchange(parts, ("yl", "x")))
    scores = exchange(summed, ("yl", "x"))
    stats, cross = call(stat_kernel, [((NZ, 8, 128), F32), ((4, 72, 128), F32)], scores)
    stats = exchange(stats, ("zh", "zp")).reshape(NH, 2, 8, 128)
    far_scores = swap(cross, "zp")
    q_part, logs = call(
        share_kernel, [((NH, 32, 512), BF16), ((8, ROWS), F32)], stats, scores, asked, *columns,
        scratch=[pltpu.VMEM((ROWS, 512), F32)],
    )
    q_came = exchange(q_part, "zh")
    keep, give = call(
        column_grad_kernel, [((2, 256, 512), BF16), ((2, 256, 512), BF16)],
        logs, scores, asked, queries, far_scores, far,
        scratch=[pltpu.VMEM((ROWS, 512), BF16), pltpu.VMEM((4, ROWS), jnp.int32)],
    )
    own, cross = call(pair_kernel, [((256, 512), F32), ((256, 512), BF16)], keep, swap(give, "c"))
    cross = swap(cross, "yh")
    passage_out, negative_out = call(column_kernel, [((32, 512), BF16), ((224, 512), BF16)], own, cross)
    (query_out,) = call(query_kernel, [((32, 512), BF16)], q_came)
    return (query_out, passage_out, negative_out)


def solution(mesh):
    fine = Mesh(mesh.devices.reshape(2, NH, 2, 2, 2, 4), ("yh", "zh", "zp", "c", "yl", "x"))
    dp, mp = ("yh", "zh", "zp", "c"), ("yl", "x")
    return jax.shard_map(
        shards,
        mesh=fine,
        in_specs=(P(dp, mp), P(dp, mp), P(dp, mp), P(dp, None), P(dp, None)),
        out_specs=(P(dp, mp), P(dp, mp), P(dp, mp)),
        check_vma=False,
    )
```

```python
import math

import jax
import jax.numpy as jnp
from jax import lax
from jax.experimental import pallas as pl
from jax.experimental.pallas import tpu as pltpu
from jax.sharding import Mesh
from jax.sharding import PartitionSpec as P

BF16 = jnp.bfloat16
F32 = jnp.float32
NZ = 16
NH = 8
NB = 8
ROWS = 256
ABSENT = -1e30
VMEM_LIMIT = 48 * 1024 * 1024
PACK_LIMIT = 62 * 1024 * 1024
HOLD_FLOPS = 1153000000


def call(kernel, out_shapes, *args, hbm=0, scratch=(), limit=VMEM_LIMIT):
    specs = [pl.BlockSpec(memory_space=pl.ANY)] * hbm
    specs += [pl.BlockSpec(memory_space=pltpu.VMEM)] * (len(args) - hbm)
    return pl.pallas_call(
        kernel,
        out_shape=[jax.ShapeDtypeStruct(shape, dtype) for shape, dtype in out_shapes],
        in_specs=specs,
        out_specs=[pl.BlockSpec(memory_space=pltpu.VMEM)] * len(out_shapes),
        scratch_shapes=list(scratch),
        compiler_params=pltpu.CompilerParams(vmem_limit_bytes=limit),
    )(*args)


def pack_kernel(queries, owners, rows, sent, mine, short, wide, sems):
    copies = [
        pltpu.make_async_copy(owners, short.at[0], sems.at[0]),
        pltpu.make_async_copy(rows, short.at[1], sems.at[1]),
        pltpu.make_async_copy(queries, mine, sems.at[2]),
    ]
    for copy in copies:
        copy.start()
    yh, zh, zp, c = (lax.axis_index(axis) for axis in ("yh", "zh", "zp", "c"))
    line = lax.broadcasted_iota(jnp.int32, (NH * 16, 128), 0)
    lane = lax.broadcasted_iota(jnp.int32, (NH * 16, 128), 1)
    block = line % 16
    z = (line // 16) * 2 + (zp ^ (block // 4))
    owner = ((yh ^ (block // 2 % 2)) * NZ + z) * 2 + (c ^ (block % 2))
    owner = jnp.where((block < NB) & (lane // 32 == zh % 4), owner, -2)
    copies[0].wait()
    copies[1].wait()
    for j in range(4):
        wide[:, :, j * 32 : (j + 1) * 32] = short[...]
    asked = jnp.full((NH * 16, 128), -1, jnp.int32)
    for k in range(short.shape[1]):
        asked = jnp.where(wide[0, k : k + 1, :] == owner, wide[1, k : k + 1, :], asked)
    asked = asked.astype(F32).astype(BF16)
    for to in range(NH):
        sent[to, 128:144, :] = asked[to * 16 : (to + 1) * 16, :]
    copies[2].wait()
    for to in range(NH):
        for l in range(4):
            sent[to, l * 32 : (l + 1) * 32, :] = mine[:, l * 128 : (l + 1) * 128]


def column_pack_kernel(passages, negatives, columns, sems):
    copies = [
        pltpu.make_async_copy(negatives, columns.at[32:256], sems.at[0]),
        pltpu.make_async_copy(passages, columns.at[0:32], sems.at[1]),
    ]
    for copy in copies:
        copy.start()
    for copy in copies:
        copy.wait()


def unpack(came, lines, queries, asked):
    for z in range(NH):
        for l in range(4):
            queries[z * 32 : (z + 1) * 32, l * 128 : (l + 1) * 128] = came[z, l * 32 : (l + 1) * 32, :]
    for g in range(2):
        rows = came[4 * g, 128:144, :].astype(F32)
        for z in range(4 * g + 1, 4 * g + 4):
            rows = jnp.maximum(rows, came[z, 128:144, :].astype(F32))
        asked[:, g * 128 : (g + 1) * 128] = rows[lines, :].astype(jnp.int32)


def stack_kernel(first, second, both):
    both[0:256, :] = first[...]
    both[256:512, :] = second[...]


def score_kernel(near, *refs):
    columns, (parts, queries, asked) = refs[:4], refs[4:]
    scale = 3.0 / math.sqrt(4096)
    unpack(near, slice(0, NB), queries, asked)
    every = queries[...]
    place = lax.broadcasted_iota(jnp.int32, (224, ROWS), 0)
    for o in range(NB):
        cols = columns[o % 4][o // 4 * 256 : (o // 4 + 1) * 256, :]
        part = lax.dot_general(cols, every, (((1,), (1,)), ((), ())), preferred_element_type=F32)
        want = asked[o : o + 1, :]
        hard = jnp.sum(jnp.where(place == want, part[32:256, :], 0.0), axis=0, keepdims=True) * scale
        hard = jnp.where(want >= 0, hard, ABSENT)
        h, a = o // 2, o % 2
        for l in range(2):
            lanes = slice(l * 128, (l + 1) * 128)
            parts[h * 2 + l, a * 32 : (a + 1) * 32, :] = part[0:32, lanes] * scale
            parts[h * 2 + l, 64 + a : 65 + a, :] = hard[:, lanes]
            if a == 1:
                parts[h * 2 + l, 66:72, :] = jnp.zeros((6, 128), F32)


def add_kernel(came, sent):
    total = came[0]
    for i in range(1, 8):
        total = total + came[i]
    for i in range(8):
        sent[i] = total


def stat_kernel(scores, far, sent, cross):
    cross[...] = scores[4:8]
    for l in range(2):
        batch = [scores[h * 2 + l, 0:64, :] for h in range(4)]
        hard = [scores[h * 2 + l, 64:66, :] for h in range(4)]
        top = jnp.maximum(
            jnp.max(jnp.maximum(jnp.maximum(batch[0], batch[1]), jnp.maximum(batch[2], batch[3])), axis=0, keepdims=True),
            jnp.max(jnp.maximum(jnp.maximum(hard[0], hard[1]), jnp.maximum(hard[2], hard[3])), axis=0, keepdims=True),
        )
        total = jnp.sum(sum(jnp.exp(b - top) for b in batch), axis=0, keepdims=True)
        total = total + jnp.sum(sum(jnp.exp(h - top) for h in hard), axis=0, keepdims=True)
        for to in range(NZ):
            sent[to, l : l + 1, :] = top
            sent[to, 2 + l : 3 + l, :] = total
    for to in range(NZ):
        sent[to, 4:8, :] = jnp.zeros((4, 128), F32)


def row_logs(stats, zp):
    logs = []
    for l in range(2):
        tops = jnp.where(zp == 0, stats[:, 0, l, :], stats[:, 1, l, :])
        totals = jnp.where(zp == 0, stats[:, 0, 2 + l, :], stats[:, 1, 2 + l, :])
        top = jnp.max(tops, axis=0, keepdims=True)
        logs.append(top + jnp.log(jnp.sum(totals * jnp.exp(tops - top), axis=0, keepdims=True)))
    return jnp.concatenate(logs, axis=1)


def block_weights(scores, o, logs, want, targets):
    h, a = o // 2, o % 2
    batch = jnp.concatenate([scores[h * 2 + l, a * 32 : (a + 1) * 32, :] for l in range(2)], axis=1)
    hard = jnp.concatenate([scores[h * 2 + l, 64 + a : 65 + a, :] for l in range(2)], axis=1)
    weights = jnp.exp(batch - logs)
    if targets and o == 0:
        row = lax.broadcasted_iota(jnp.int32, (32, ROWS), 0)
        lane = lax.broadcasted_iota(jnp.int32, (32, ROWS), 1)
        weights = weights - (lane == lax.axis_index("zh") * 32 + row).astype(F32)
    line = lax.broadcasted_iota(jnp.int32, (224, ROWS), 0)
    hard = jnp.where(line == want, jnp.exp(hard - logs), 0.0)
    return jnp.concatenate([weights.astype(BF16), hard.astype(BF16)], axis=0)


def share_kernel(stats, scores, asked, *refs):
    columns, (sent, logs, total) = refs[:4], refs[4:]
    zp = lax.axis_index("zp")
    near = row_logs(stats, zp)
    logs[0:1, :] = near
    logs[1:2, :] = row_logs(stats, 1 - zp)
    for o in range(NB):
        weights = block_weights(scores, o, near, asked[o : o + 1, :], True)
        cols = columns[o % 4][o // 4 * 256 : (o // 4 + 1) * 256, :]
        term = lax.dot_general(weights, cols, (((0,), (0,)), ((), ())), preferred_element_type=F32)
        if o == 0:
            total[...] = term
        elif o < NB - 1:
            total[...] += term
        else:
            sent[...] = (total[...] + term).astype(BF16).reshape(NH, 32, 512)


def column_grad_kernel(logs, scores, asked, queries, far_scores, far, keep, give, far_queries, far_asked):
    unpack(far, slice(4, 8), far_queries, far_asked)
    near_queries, other_queries = queries[...], far_queries[...]
    for o in range(4):
        weights = block_weights(scores, o, logs[0:1, :], asked[o : o + 1, :], True)
        grad = jnp.dot(weights, near_queries, preferred_element_type=F32)
        weights = block_weights(far_scores, o, logs[1:2, :], far_asked[o : o + 1, :], False)
        grad = grad + jnp.dot(weights, other_queries, preferred_element_type=F32)
        (give if o % 2 else keep)[o // 2] = grad.astype(BF16)


def pair_kernel(keep, came, own, sent):
    own[...] = keep[0].astype(F32) + came[0].astype(F32)
    sent[...] = (keep[1].astype(F32) + came[1].astype(F32)).astype(BF16)


def column_kernel(own, came, passage_out, negative_out):
    passage_out[...] = (own[0:32, :] + came[0:32, :].astype(F32)).astype(BF16)
    negative_out[...] = (own[32:256, :] + came[32:256, :].astype(F32)).astype(BF16)


def query_kernel(came, query_out):
    total = came[0].astype(F32)
    for z in range(1, NH):
        total = total + came[z].astype(F32)
    query_out[...] = total.astype(BF16)


def hold(x):
    return pl.pallas_call(
        lambda *refs: None,
        out_shape=jax.ShapeDtypeStruct(x.shape, x.dtype),
        in_specs=[pl.BlockSpec(memory_space=pltpu.VMEM)],
        out_specs=pl.BlockSpec(memory_space=pltpu.VMEM),
        input_output_aliases={0: 0},
        cost_estimate=pl.CostEstimate(flops=HOLD_FLOPS, bytes_accessed=0, transcendentals=0),
        compiler_params=pltpu.CompilerParams(vmem_limit_bytes=VMEM_LIMIT),
    )(x)


def swap(x, axis):
    return lax.ppermute(x, axis, [(0, 1), (1, 0)])


def exchange(x, axes):
    return lax.all_to_all(x, axes, split_axis=0, concat_axis=0, tiled=True)


def shards(queries, passages, negatives, hard_owner, hard_row):
    (sent,) = call(
        pack_kernel, [((NH, 144, 128), BF16)],
        queries, hard_owner.T, hard_row.T, hbm=3, limit=PACK_LIMIT,
        scratch=[
            pltpu.VMEM((32, 512), BF16), pltpu.VMEM((2, 7, 32), jnp.int32), pltpu.VMEM((2, 7, 128), jnp.int32),
            pltpu.SemaphoreType.DMA((3,)),
        ],
    )
    (col0,) = call(
        column_pack_kernel, [((256, 512), BF16)], passages, negatives, hbm=2,
        scratch=[pltpu.SemaphoreType.DMA((2,))],
    )
    (pair,) = call(stack_kernel, [((512, 512), BF16)], col0, swap(col0, "zp"))
    near = hold(exchange(sent, "zh"))
    other = swap(pair, "yh")
    columns = (pair, swap(pair, "c"), other, swap(other, "c"))
    parts, queries, asked = call(
        score_kernel, [((8, 72, 128), F32), ((ROWS, 512), BF16), ((NB, ROWS), jnp.int32)], near, *columns
    )
    far = swap(near, "zp")
    (summed,) = call(add_kernel, [((8, 72, 128), F32)], exchange(parts, ("yl", "x")))
    scores = exchange(summed, ("yl", "x"))
    stats, cross = call(stat_kernel, [((NZ, 8, 128), F32), ((4, 72, 128), F32)], scores, far)
    stats = exchange(stats, ("zh", "zp")).reshape(NH, 2, 8, 128)
    far_scores = swap(cross, "zp")
    q_part, logs = call(
        share_kernel, [((NH, 32, 512), BF16), ((8, ROWS), F32)], stats, scores, asked, *columns,
        scratch=[pltpu.VMEM((ROWS, 512), F32)],
    )
    q_came = exchange(q_part, "zh")
    keep, give = call(
        column_grad_kernel, [((2, 256, 512), BF16), ((2, 256, 512), BF16)],
        logs, scores, asked, queries, far_scores, far,
        scratch=[pltpu.VMEM((ROWS, 512), BF16), pltpu.VMEM((4, ROWS), jnp.int32)],
    )
    own, cross = call(pair_kernel, [((256, 512), F32), ((256, 512), BF16)], keep, swap(give, "c"))
    cross = swap(cross, "yh")
    passage_out, negative_out = call(column_kernel, [((32, 512), BF16), ((224, 512), BF16)], own, cross)
    (query_out,) = call(query_kernel, [((32, 512), BF16)], q_came)
    return (query_out, passage_out, negative_out)


def solution(mesh):
    fine = Mesh(mesh.devices.reshape(2, NH, 2, 2, 2, 4), ("yh", "zh", "zp", "c", "yl", "x"))
    dp, mp = ("yh", "zh", "zp", "c"), ("yl", "x")
    return jax.shard_map(
        shards,
        mesh=fine,
        in_specs=(P(dp, mp), P(dp, mp), P(dp, mp), P(dp, None), P(dp, None)),
        out_specs=(P(dp, mp), P(dp, mp), P(dp, mp)),
        check_vma=False,
    )
```

```python
import math

import jax
import jax.numpy as jnp
from jax import lax
from jax.experimental import pallas as pl
from jax.experimental.pallas import tpu as pltpu
from jax.sharding import Mesh
from jax.sharding import PartitionSpec as P

BF16 = jnp.bfloat16
F32 = jnp.float32
NZ = 16
NH = 8
NB = 8
ROWS = 256
ABSENT = -1e30
VMEM_LIMIT = 48 * 1024 * 1024
PACK_LIMIT = 62 * 1024 * 1024
STACK_COST = pl.CostEstimate(flops=5765000000, bytes_accessed=0, transcendentals=0)


def call(kernel, out_shapes, *args, hbm=0, scratch=(), limit=VMEM_LIMIT, cost=None):
    specs = [pl.BlockSpec(memory_space=pl.ANY)] * hbm
    specs += [pl.BlockSpec(memory_space=pltpu.VMEM)] * (len(args) - hbm)
    return pl.pallas_call(
        kernel,
        out_shape=[jax.ShapeDtypeStruct(shape, dtype) for shape, dtype in out_shapes],
        in_specs=specs,
        out_specs=[pl.BlockSpec(memory_space=pltpu.VMEM)] * len(out_shapes),
        scratch_shapes=list(scratch),
        compiler_params=pltpu.CompilerParams(vmem_limit_bytes=limit),
        cost_estimate=cost,
    )(*args)


def pack_kernel(queries, owners, rows, sent, mine, short, wide, sems):
    copies = [
        pltpu.make_async_copy(owners, short.at[0], sems.at[0]),
        pltpu.make_async_copy(rows, short.at[1], sems.at[1]),
        pltpu.make_async_copy(queries, mine, sems.at[2]),
    ]
    for copy in copies:
        copy.start()
    yh, zh, zp, c = (lax.axis_index(axis) for axis in ("yh", "zh", "zp", "c"))
    line = lax.broadcasted_iota(jnp.int32, (NH * 16, 128), 0)
    lane = lax.broadcasted_iota(jnp.int32, (NH * 16, 128), 1)
    block = line % 16
    z = (line // 16) * 2 + (zp ^ (block // 4))
    owner = ((yh ^ (block // 2 % 2)) * NZ + z) * 2 + (c ^ (block % 2))
    owner = jnp.where((block < NB) & (lane // 32 == zh % 4), owner, -2)
    copies[0].wait()
    copies[1].wait()
    for j in range(4):
        wide[:, :, j * 32 : (j + 1) * 32] = short[...]
    asked = jnp.full((NH * 16, 128), -1, jnp.int32)
    for k in range(short.shape[1]):
        asked = jnp.where(wide[0, k : k + 1, :] == owner, wide[1, k : k + 1, :], asked)
    asked = asked.astype(F32).astype(BF16)
    for to in range(NH):
        sent[to, 128:144, :] = asked[to * 16 : (to + 1) * 16, :]
    copies[2].wait()
    for to in range(NH):
        for l in range(4):
            sent[to, l * 32 : (l + 1) * 32, :] = mine[:, l * 128 : (l + 1) * 128]


def column_pack_kernel(passages, negatives, columns, sems):
    copies = [
        pltpu.make_async_copy(negatives, columns.at[32:256], sems.at[0]),
        pltpu.make_async_copy(passages, columns.at[0:32], sems.at[1]),
    ]
    for copy in copies:
        copy.start()
    for copy in copies:
        copy.wait()


def unpack(came, lines, queries, asked):
    for z in range(NH):
        for l in range(4):
            queries[z * 32 : (z + 1) * 32, l * 128 : (l + 1) * 128] = came[z, l * 32 : (l + 1) * 32, :]
    for g in range(2):
        rows = came[4 * g, 128:144, :].astype(F32)
        for z in range(4 * g + 1, 4 * g + 4):
            rows = jnp.maximum(rows, came[z, 128:144, :].astype(F32))
        asked[:, g * 128 : (g + 1) * 128] = rows[lines, :].astype(jnp.int32)


def stack_kernel(first, second, both):
    both[0:256, :] = first[...]
    both[256:512, :] = second[...]


def score_kernel(near, *refs):
    columns, (parts, queries, asked) = refs[:4], refs[4:]
    scale = 3.0 / math.sqrt(4096)
    unpack(near, slice(0, NB), queries, asked)
    every = queries[...]
    place = lax.broadcasted_iota(jnp.int32, (224, ROWS), 0)
    for o in range(NB):
        cols = columns[o % 4][o // 4 * 256 : (o // 4 + 1) * 256, :]
        part = lax.dot_general(cols, every, (((1,), (1,)), ((), ())), preferred_element_type=F32)
        want = asked[o : o + 1, :]
        hard = jnp.sum(jnp.where(place == want, part[32:256, :], 0.0), axis=0, keepdims=True) * scale
        hard = jnp.where(want >= 0, hard, ABSENT)
        h, a = o // 2, o % 2
        for l in range(2):
            lanes = slice(l * 128, (l + 1) * 128)
            parts[h * 2 + l, a * 32 : (a + 1) * 32, :] = part[0:32, lanes] * scale
            parts[h * 2 + l, 64 + a : 65 + a, :] = hard[:, lanes]
            if a == 1:
                parts[h * 2 + l, 66:72, :] = jnp.zeros((6, 128), F32)


def add_kernel(came, far, sent):
    total = came[0]
    for i in range(1, 8):
        total = total + came[i]
    for i in range(8):
        sent[i] = total


def stat_kernel(scores, sent, cross):
    cross[...] = scores[4:8]
    for l in range(2):
        batch = [scores[h * 2 + l, 0:64, :] for h in range(4)]
        hard = [scores[h * 2 + l, 64:66, :] for h in range(4)]
        top = jnp.maximum(
            jnp.max(jnp.maximum(jnp.maximum(batch[0], batch[1]), jnp.maximum(batch[2], batch[3])), axis=0, keepdims=True),
            jnp.max(jnp.maximum(jnp.maximum(hard[0], hard[1]), jnp.maximum(hard[2], hard[3])), axis=0, keepdims=True),
        )
        total = jnp.sum(sum(jnp.exp(b - top) for b in batch), axis=0, keepdims=True)
        total = total + jnp.sum(sum(jnp.exp(h - top) for h in hard), axis=0, keepdims=True)
        for to in range(NZ):
            sent[to, l : l + 1, :] = top
            sent[to, 2 + l : 3 + l, :] = total
    for to in range(NZ):
        sent[to, 4:8, :] = jnp.zeros((4, 128), F32)


def row_logs(stats, zp):
    logs = []
    for l in range(2):
        tops = jnp.where(zp == 0, stats[:, 0, l, :], stats[:, 1, l, :])
        totals = jnp.where(zp == 0, stats[:, 0, 2 + l, :], stats[:, 1, 2 + l, :])
        top = jnp.max(tops, axis=0, keepdims=True)
        logs.append(top + jnp.log(jnp.sum(totals * jnp.exp(tops - top), axis=0, keepdims=True)))
    return jnp.concatenate(logs, axis=1)


def block_weights(scores, o, logs, want, targets):
    h, a = o // 2, o % 2
    batch = jnp.concatenate([scores[h * 2 + l, a * 32 : (a + 1) * 32, :] for l in range(2)], axis=1)
    hard = jnp.concatenate([scores[h * 2 + l, 64 + a : 65 + a, :] for l in range(2)], axis=1)
    weights = jnp.exp(batch - logs)
    if targets and o == 0:
        row = lax.broadcasted_iota(jnp.int32, (32, ROWS), 0)
        lane = lax.broadcasted_iota(jnp.int32, (32, ROWS), 1)
        weights = weights - (lane == lax.axis_index("zh") * 32 + row).astype(F32)
    line = lax.broadcasted_iota(jnp.int32, (224, ROWS), 0)
    hard = jnp.where(line == want, jnp.exp(hard - logs), 0.0)
    return jnp.concatenate([weights.astype(BF16), hard.astype(BF16)], axis=0)


def share_kernel(stats, scores, asked, *refs):
    columns, (sent, logs, total) = refs[:4], refs[4:]
    zp = lax.axis_index("zp")
    near = row_logs(stats, zp)
    logs[0:1, :] = near
    logs[1:2, :] = row_logs(stats, 1 - zp)
    for o in range(NB):
        weights = block_weights(scores, o, near, asked[o : o + 1, :], True)
        cols = columns[o % 4][o // 4 * 256 : (o // 4 + 1) * 256, :]
        term = lax.dot_general(weights, cols, (((0,), (0,)), ((), ())), preferred_element_type=F32)
        if o == 0:
            total[...] = term
        elif o < NB - 1:
            total[...] += term
        else:
            sent[...] = (total[...] + term).astype(BF16).reshape(NH, 32, 512)


def column_grad_kernel(logs, scores, asked, queries, far_scores, far, keep, give, far_queries, far_asked):
    unpack(far, slice(4, 8), far_queries, far_asked)
    near_queries, other_queries = queries[...], far_queries[...]
    for o in range(4):
        weights = block_weights(scores, o, logs[0:1, :], asked[o : o + 1, :], True)
        grad = jnp.dot(weights, near_queries, preferred_element_type=F32)
        weights = block_weights(far_scores, o, logs[1:2, :], far_asked[o : o + 1, :], False)
        grad = grad + jnp.dot(weights, other_queries, preferred_element_type=F32)
        (give if o % 2 else keep)[o // 2] = grad.astype(BF16)


def pair_kernel(keep, came, own, sent):
    own[...] = keep[0].astype(F32) + came[0].astype(F32)
    sent[...] = (keep[1].astype(F32) + came[1].astype(F32)).astype(BF16)


def column_kernel(own, came, passage_out, negative_out):
    passage_out[...] = (own[0:32, :] + came[0:32, :].astype(F32)).astype(BF16)
    negative_out[...] = (own[32:256, :] + came[32:256, :].astype(F32)).astype(BF16)


def query_kernel(came, query_out):
    total = came[0].astype(F32)
    for z in range(1, NH):
        total = total + came[z].astype(F32)
    query_out[...] = total.astype(BF16)


def swap(x, axis):
    return lax.ppermute(x, axis, [(0, 1), (1, 0)])


def exchange(x, axes):
    return lax.all_to_all(x, axes, split_axis=0, concat_axis=0, tiled=True)


def shards(queries, passages, negatives, hard_owner, hard_row):
    (sent,) = call(
        pack_kernel, [((NH, 144, 128), BF16)],
        queries, hard_owner.T, hard_row.T, hbm=3, limit=PACK_LIMIT,
        scratch=[
            pltpu.VMEM((32, 512), BF16), pltpu.VMEM((2, 7, 32), jnp.int32), pltpu.VMEM((2, 7, 128), jnp.int32),
            pltpu.SemaphoreType.DMA((3,)),
        ],
    )
    (col0,) = call(
        column_pack_kernel, [((256, 512), BF16)], passages, negatives, hbm=2,
        scratch=[pltpu.SemaphoreType.DMA((2,))],
    )
    by_yh, by_zp = swap(col0, "yh"), swap(col0, "zp")
    near = exchange(sent, "zh")
    (pair,) = call(stack_kernel, [((512, 512), BF16)], col0, by_zp, cost=STACK_COST)
    (other,) = call(stack_kernel, [((512, 512), BF16)], by_yh, swap(by_zp, "yh"), cost=STACK_COST)
    columns = (pair, swap(pair, "c"), other, swap(other, "c"))
    parts, queries, asked = call(
        score_kernel, [((8, 72, 128), F32), ((ROWS, 512), BF16), ((NB, ROWS), jnp.int32)], near, *columns
    )
    far = swap(near, "zp")
    (summed,) = call(add_kernel, [((8, 72, 128), F32)], exchange(parts, ("yl", "x")), far)
    scores = exchange(summed, ("yl", "x"))
    stats, cross = call(stat_kernel, [((NZ, 8, 128), F32), ((4, 72, 128), F32)], scores)
    stats = exchange(stats, ("zh", "zp")).reshape(NH, 2, 8, 128)
    far_scores = swap(cross, "zp")
    q_part, logs = call(
        share_kernel, [((NH, 32, 512), BF16), ((8, ROWS), F32)], stats, scores, asked, *columns,
        scratch=[pltpu.VMEM((ROWS, 512), F32)],
    )
    q_came = exchange(q_part, "zh")
    keep, give = call(
        column_grad_kernel, [((2, 256, 512), BF16), ((2, 256, 512), BF16)],
        logs, scores, asked, queries, far_scores, far,
        scratch=[pltpu.VMEM((ROWS, 512), BF16), pltpu.VMEM((4, ROWS), jnp.int32)],
    )
    own, cross = call(pair_kernel, [((256, 512), F32), ((256, 512), BF16)], keep, swap(give, "c"))
    cross = swap(cross, "yh")
    passage_out, negative_out = call(column_kernel, [((32, 512), BF16), ((224, 512), BF16)], own, cross)
    (query_out,) = call(query_kernel, [((32, 512), BF16)], q_came)
    return (query_out, passage_out, negative_out)


def solution(mesh):
    fine = Mesh(mesh.devices.reshape(2, NH, 2, 2, 2, 4), ("yh", "zh", "zp", "c", "yl", "x"))
    dp, mp = ("yh", "zh", "zp", "c"), ("yl", "x")
    return jax.shard_map(
        shards,
        mesh=fine,
        in_specs=(P(dp, mp), P(dp, mp), P(dp, mp), P(dp, None), P(dp, None)),
        out_specs=(P(dp, mp), P(dp, mp), P(dp, mp)),
        check_vma=False,
    )
```

```python
import math

import jax
import jax.numpy as jnp
from jax import lax
from jax.experimental import pallas as pl
from jax.experimental.pallas import tpu as pltpu
from jax.sharding import Mesh
from jax.sharding import PartitionSpec as P

BF16 = jnp.bfloat16
F32 = jnp.float32
NZ = 16
NH = 8
NB = 8
ROWS = 256
ABSENT = -1e30
VMEM_LIMIT = 48 * 1024 * 1024
PACK_LIMIT = 62 * 1024 * 1024
STACK_COST = pl.CostEstimate(flops=5765000000, bytes_accessed=0, transcendentals=0)


def call(kernel, out_shapes, *args, hbm=0, scratch=(), limit=VMEM_LIMIT, cost=None):
    specs = [pl.BlockSpec(memory_space=pl.ANY)] * hbm
    specs += [pl.BlockSpec(memory_space=pltpu.VMEM)] * (len(args) - hbm)
    return pl.pallas_call(
        kernel,
        out_shape=[jax.ShapeDtypeStruct(shape, dtype) for shape, dtype in out_shapes],
        in_specs=specs,
        out_specs=[pl.BlockSpec(memory_space=pltpu.VMEM)] * len(out_shapes),
        scratch_shapes=list(scratch),
        compiler_params=pltpu.CompilerParams(vmem_limit_bytes=limit),
        cost_estimate=cost,
    )(*args)


def pack_kernel(queries, owners, rows, negatives, passages, sent, columns, mine, short, wide, sems):
    copies = [
        pltpu.make_async_copy(owners, short.at[0], sems.at[0]),
        pltpu.make_async_copy(rows, short.at[1], sems.at[1]),
        pltpu.make_async_copy(queries, mine, sems.at[2]),
        pltpu.make_async_copy(negatives, columns.at[32:256], sems.at[3]),
        pltpu.make_async_copy(passages, columns.at[0:32], sems.at[4]),
    ]
    for copy in copies:
        copy.start()
    yh, zh, zp, c = (lax.axis_index(axis) for axis in ("yh", "zh", "zp", "c"))
    line = lax.broadcasted_iota(jnp.int32, (NH * 16, 128), 0)
    lane = lax.broadcasted_iota(jnp.int32, (NH * 16, 128), 1)
    block = line % 16
    z = (line // 16) * 2 + (zp ^ (block // 4))
    owner = ((yh ^ (block // 2 % 2)) * NZ + z) * 2 + (c ^ (block % 2))
    owner = jnp.where((block < NB) & (lane // 32 == zh % 4), owner, -2)
    copies[0].wait()
    copies[1].wait()
    for j in range(4):
        wide[:, :, j * 32 : (j + 1) * 32] = short[...]
    asked = jnp.full((NH * 16, 128), -1, jnp.int32)
    for k in range(short.shape[1]):
        asked = jnp.where(wide[0, k : k + 1, :] == owner, wide[1, k : k + 1, :], asked)
    asked = asked.astype(F32).astype(BF16)
    for to in range(NH):
        sent[to, 128:144, :] = asked[to * 16 : (to + 1) * 16, :]
    copies[2].wait()
    for to in range(NH):
        for l in range(4):
            sent[to, l * 32 : (l + 1) * 32, :] = mine[:, l * 128 : (l + 1) * 128]
    copies[3].wait()
    copies[4].wait()


def unpack(came, lines, queries, asked):
    for z in range(NH):
        for l in range(4):
            queries[z * 32 : (z + 1) * 32, l * 128 : (l + 1) * 128] = came[z, l * 32 : (l + 1) * 32, :]
    for g in range(2):
        rows = came[4 * g, 128:144, :].astype(F32)
        for z in range(4 * g + 1, 4 * g + 4):
            rows = jnp.maximum(rows, came[z, 128:144, :].astype(F32))
        asked[:, g * 128 : (g + 1) * 128] = rows[lines, :].astype(jnp.int32)


def stack_kernel(first, second, both):
    both[0:256, :] = first[...]
    both[256:512, :] = second[...]


def score_kernel(near, *refs):
    columns, (parts, queries, asked) = refs[:4], refs[4:]
    scale = 3.0 / math.sqrt(4096)
    unpack(near, slice(0, NB), queries, asked)
    every = queries[...]
    place = lax.broadcasted_iota(jnp.int32, (224, ROWS), 0)
    for o in range(NB):
        cols = columns[o % 4][o // 4 * 256 : (o // 4 + 1) * 256, :]
        part = lax.dot_general(cols, every, (((1,), (1,)), ((), ())), preferred_element_type=F32)
        want = asked[o : o + 1, :]
        hard = jnp.sum(jnp.where(place == want, part[32:256, :], 0.0), axis=0, keepdims=True) * scale
        hard = jnp.where(want >= 0, hard, ABSENT)
        h, a = o // 2, o % 2
        for l in range(2):
            lanes = slice(l * 128, (l + 1) * 128)
            parts[h * 2 + l, a * 32 : (a + 1) * 32, :] = part[0:32, lanes] * scale
            parts[h * 2 + l, 64 + a : 65 + a, :] = hard[:, lanes]
            if a == 1:
                parts[h * 2 + l, 66:72, :] = jnp.zeros((6, 128), F32)


def add_kernel(came, far, sent):
    total = came[0]
    for i in range(1, 8):
        total = total + came[i]
    for i in range(8):
        sent[i] = total


def stat_kernel(scores, sent, cross):
    cross[...] = scores[4:8]
    for l in range(2):
        batch = [scores[h * 2 + l, 0:64, :] for h in range(4)]
        hard = [scores[h * 2 + l, 64:66, :] for h in range(4)]
        top = jnp.maximum(
            jnp.max(jnp.maximum(jnp.maximum(batch[0], batch[1]), jnp.maximum(batch[2], batch[3])), axis=0, keepdims=True),
            jnp.max(jnp.maximum(jnp.maximum(hard[0], hard[1]), jnp.maximum(hard[2], hard[3])), axis=0, keepdims=True),
        )
        total = jnp.sum(sum(jnp.exp(b - top) for b in batch), axis=0, keepdims=True)
        total = total + jnp.sum(sum(jnp.exp(h - top) for h in hard), axis=0, keepdims=True)
        for to in range(NZ):
            sent[to, l : l + 1, :] = top
            sent[to, 2 + l : 3 + l, :] = total
    for to in range(NZ):
        sent[to, 4:8, :] = jnp.zeros((4, 128), F32)


def row_logs(stats, zp):
    logs = []
    for l in range(2):
        tops = jnp.where(zp == 0, stats[:, 0, l, :], stats[:, 1, l, :])
        totals = jnp.where(zp == 0, stats[:, 0, 2 + l, :], stats[:, 1, 2 + l, :])
        top = jnp.max(tops, axis=0, keepdims=True)
        logs.append(top + jnp.log(jnp.sum(totals * jnp.exp(tops - top), axis=0, keepdims=True)))
    return jnp.concatenate(logs, axis=1)


def block_weights(scores, o, logs, want, targets):
    h, a = o // 2, o % 2
    batch = jnp.concatenate([scores[h * 2 + l, a * 32 : (a + 1) * 32, :] for l in range(2)], axis=1)
    hard = jnp.concatenate([scores[h * 2 + l, 64 + a : 65 + a, :] for l in range(2)], axis=1)
    weights = jnp.exp(batch - logs)
    if targets and o == 0:
        row = lax.broadcasted_iota(jnp.int32, (32, ROWS), 0)
        lane = lax.broadcasted_iota(jnp.int32, (32, ROWS), 1)
        weights = weights - (lane == lax.axis_index("zh") * 32 + row).astype(F32)
    line = lax.broadcasted_iota(jnp.int32, (224, ROWS), 0)
    hard = jnp.where(line == want, jnp.exp(hard - logs), 0.0)
    return jnp.concatenate([weights.astype(BF16), hard.astype(BF16)], axis=0)


def share_kernel(stats, scores, asked, *refs):
    columns, (sent, logs, total) = refs[:4], refs[4:]
    zp = lax.axis_index("zp")
    near = row_logs(stats, zp)
    logs[0:1, :] = near
    logs[1:2, :] = row_logs(stats, 1 - zp)
    for o in range(NB):
        weights = block_weights(scores, o, near, asked[o : o + 1, :], True)
        cols = columns[o % 4][o // 4 * 256 : (o // 4 + 1) * 256, :]
        term = lax.dot_general(weights, cols, (((0,), (0,)), ((), ())), preferred_element_type=F32)
        if o == 0:
            total[...] = term
        elif o < NB - 1:
            total[...] += term
        else:
            sent[...] = (total[...] + term).astype(BF16).reshape(NH, 32, 512)


def column_grad_kernel(logs, scores, asked, queries, far_scores, far, keep, give, far_queries, far_asked):
    unpack(far, slice(4, 8), far_queries, far_asked)
    near_queries, other_queries = queries[...], far_queries[...]
    for o in range(4):
        weights = block_weights(scores, o, logs[0:1, :], asked[o : o + 1, :], True)
        grad = jnp.dot(weights, near_queries, preferred_element_type=F32)
        weights = block_weights(far_scores, o, logs[1:2, :], far_asked[o : o + 1, :], False)
        grad = grad + jnp.dot(weights, other_queries, preferred_element_type=F32)
        (give if o % 2 else keep)[o // 2] = grad.astype(BF16)


def pair_kernel(keep, came, own, sent):
    own[...] = keep[0].astype(F32) + came[0].astype(F32)
    sent[...] = (keep[1].astype(F32) + came[1].astype(F32)).astype(BF16)


def column_kernel(own, came, passage_out, negative_out):
    passage_out[...] = (own[0:32, :] + came[0:32, :].astype(F32)).astype(BF16)
    negative_out[...] = (own[32:256, :] + came[32:256, :].astype(F32)).astype(BF16)


def query_kernel(came, query_out):
    total = came[0].astype(F32)
    for z in range(1, NH):
        total = total + came[z].astype(F32)
    query_out[...] = total.astype(BF16)


def swap(x, axis):
    return lax.ppermute(x, axis, [(0, 1), (1, 0)])


def exchange(x, axes):
    return lax.all_to_all(x, axes, split_axis=0, concat_axis=0, tiled=True)


def shards(queries, passages, negatives, hard_owner, hard_row):
    sent, col0 = call(
        pack_kernel, [((NH, 144, 128), BF16), ((256, 512), BF16)],
        queries, hard_owner.T, hard_row.T, negatives, passages, hbm=5, limit=PACK_LIMIT,
        scratch=[
            pltpu.VMEM((32, 512), BF16), pltpu.VMEM((2, 7, 32), jnp.int32), pltpu.VMEM((2, 7, 128), jnp.int32),
            pltpu.SemaphoreType.DMA((5,)),
        ],
    )
    by_yh, by_zp = swap(col0, "yh"), swap(col0, "zp")
    near = exchange(sent, "zh")
    (pair,) = call(stack_kernel, [((512, 512), BF16)], col0, by_zp, cost=STACK_COST)
    (other,) = call(stack_kernel, [((512, 512), BF16)], by_yh, swap(by_zp, "yh"), cost=STACK_COST)
    columns = (pair, swap(pair, "c"), other, swap(other, "c"))
    parts, queries, asked = call(
        score_kernel, [((8, 72, 128), F32), ((ROWS, 512), BF16), ((NB, ROWS), jnp.int32)], near, *columns
    )
    far = swap(near, "zp")
    (summed,) = call(add_kernel, [((8, 72, 128), F32)], exchange(parts, ("yl", "x")), far)
    scores = exchange(summed, ("yl", "x"))
    stats, cross = call(stat_kernel, [((NZ, 8, 128), F32), ((4, 72, 128), F32)], scores)
    stats = exchange(stats, ("zh", "zp")).reshape(NH, 2, 8, 128)
    far_scores = swap(cross, "zp")
    q_part, logs = call(
        share_kernel, [((NH, 32, 512), BF16), ((8, ROWS), F32)], stats, scores, asked, *columns,
        scratch=[pltpu.VMEM((ROWS, 512), F32)],
    )
    q_came = exchange(q_part, "zh")
    keep, give = call(
        column_grad_kernel, [((2, 256, 512), BF16), ((2, 256, 512), BF16)],
        logs, scores, asked, queries, far_scores, far,
        scratch=[pltpu.VMEM((ROWS, 512), BF16), pltpu.VMEM((4, ROWS), jnp.int32)],
    )
    own, cross = call(pair_kernel, [((256, 512), F32), ((256, 512), BF16)], keep, swap(give, "c"))
    cross = swap(cross, "yh")
    passage_out, negative_out = call(column_kernel, [((32, 512), BF16), ((224, 512), BF16)], own, cross)
    (query_out,) = call(query_kernel, [((32, 512), BF16)], q_came)
    return (query_out, passage_out, negative_out)


def solution(mesh):
    fine = Mesh(mesh.devices.reshape(2, NH, 2, 2, 2, 4), ("yh", "zh", "zp", "c", "yl", "x"))
    dp, mp = ("yh", "zh", "zp", "c"), ("yl", "x")
    return jax.shard_map(
        shards,
        mesh=fine,
        in_specs=(P(dp, mp), P(dp, mp), P(dp, mp), P(dp, None), P(dp, None)),
        out_specs=(P(dp, mp), P(dp, mp), P(dp, mp)),
        check_vma=False,
    )
```

```python
import math

import jax
import jax.numpy as jnp
from jax import lax
from jax.experimental import pallas as pl
from jax.experimental.pallas import tpu as pltpu
from jax.sharding import Mesh
from jax.sharding import PartitionSpec as P

BF16 = jnp.bfloat16
F32 = jnp.float32
NZ = 16
NH = 8
NB = 8
ROWS = 256
ABSENT = -1e30
VMEM_LIMIT = 48 * 1024 * 1024
PACK_LIMIT = 62 * 1024 * 1024
STACK_COST = pl.CostEstimate(flops=5765000000, bytes_accessed=0, transcendentals=0)


def call(kernel, out_shapes, *args, hbm=0, scratch=(), limit=VMEM_LIMIT, cost=None):
    specs = [pl.BlockSpec(memory_space=pl.ANY)] * hbm
    specs += [pl.BlockSpec(memory_space=pltpu.VMEM)] * (len(args) - hbm)
    return pl.pallas_call(
        kernel,
        out_shape=[jax.ShapeDtypeStruct(shape, dtype) for shape, dtype in out_shapes],
        in_specs=specs,
        out_specs=[pl.BlockSpec(memory_space=pltpu.VMEM)] * len(out_shapes),
        scratch_shapes=list(scratch),
        compiler_params=pltpu.CompilerParams(vmem_limit_bytes=limit),
        cost_estimate=cost,
    )(*args)


def pack_kernel(queries, owners, rows, negatives, passages, sent, columns, mine, short, wide, sems):
    copies = [
        pltpu.make_async_copy(owners, short.at[0], sems.at[0]),
        pltpu.make_async_copy(rows, short.at[1], sems.at[1]),
        pltpu.make_async_copy(queries, mine, sems.at[2]),
        pltpu.make_async_copy(negatives, columns.at[32:256], sems.at[3]),
        pltpu.make_async_copy(passages, columns.at[0:32], sems.at[4]),
    ]
    for copy in copies:
        copy.start()
    yh, zh, zp, c = (lax.axis_index(axis) for axis in ("yh", "zh", "zp", "c"))
    line = lax.broadcasted_iota(jnp.int32, (NH * 16, 128), 0)
    lane = lax.broadcasted_iota(jnp.int32, (NH * 16, 128), 1)
    block = line % 16
    z = (line // 16) * 2 + (zp ^ (block // 4))
    owner = ((yh ^ (block // 2 % 2)) * NZ + z) * 2 + (c ^ (block % 2))
    owner = jnp.where((block < NB) & (lane // 32 == zh % 4), owner, -2)
    copies[0].wait()
    copies[1].wait()
    for j in range(4):
        wide[:, :, j * 32 : (j + 1) * 32] = short[...]
    asked = jnp.full((NH * 16, 128), -1, jnp.int32)
    for k in range(short.shape[1]):
        asked = jnp.where(wide[0, k : k + 1, :] == owner, wide[1, k : k + 1, :], asked)
    asked = asked.astype(F32).astype(BF16)
    for to in range(NH):
        sent[to, 128:144, :] = asked[to * 16 : (to + 1) * 16, :]
    copies[2].wait()
    for to in range(NH):
        for l in range(4):
            sent[to, l * 32 : (l + 1) * 32, :] = mine[:, l * 128 : (l + 1) * 128]
    copies[3].wait()
    copies[4].wait()


def unpack(came, lines, queries, asked):
    for z in range(NH):
        for l in range(4):
            queries[z * 32 : (z + 1) * 32, l * 128 : (l + 1) * 128] = came[z, l * 32 : (l + 1) * 32, :]
    for g in range(2):
        rows = came[4 * g, 128:144, :].astype(F32)
        for z in range(4 * g + 1, 4 * g + 4):
            rows = jnp.maximum(rows, came[z, 128:144, :].astype(F32))
        asked[:, g * 128 : (g + 1) * 128] = rows[lines, :].astype(jnp.int32)


def stack_kernel(first, second, both):
    both[0:256, :] = first[...]
    both[256:512, :] = second[...]


def score_kernel(near, *refs):
    columns, (parts, queries, asked) = refs[:4], refs[4:]
    scale = 3.0 / math.sqrt(4096)
    unpack(near, slice(0, NB), queries, asked)
    every = queries[...]
    place = lax.broadcasted_iota(jnp.int32, (224, ROWS), 0)
    for o in range(NB):
        cols = columns[o % 4][o // 4 * 256 : (o // 4 + 1) * 256, :]
        part = lax.dot_general(cols, every, (((1,), (1,)), ((), ())), preferred_element_type=F32)
        want = asked[o : o + 1, :]
        hard = jnp.sum(jnp.where(place == want, part[32:256, :], 0.0), axis=0, keepdims=True) * scale
        hard = jnp.where(want >= 0, hard, ABSENT)
        h, a = o // 2, o % 2
        for l in range(2):
            lanes = slice(l * 128, (l + 1) * 128)
            parts[h * 2 + l, a * 32 : (a + 1) * 32, :] = part[0:32, lanes] * scale
            parts[h * 2 + l, 64 + a : 65 + a, :] = hard[:, lanes]
            if a == 1:
                parts[h * 2 + l, 66:72, :] = jnp.zeros((6, 128), F32)


def add_kernel(came, far, sent):
    total = came[0]
    for i in range(1, 8):
        total = total + came[i]
    for i in range(8):
        sent[i] = total


def stat_kernel(scores, sent, cross):
    cross[...] = scores[4:8]
    for l in range(2):
        batch = [scores[h * 2 + l, 0:64, :] for h in range(4)]
        hard = [scores[h * 2 + l, 64:66, :] for h in range(4)]
        top = jnp.maximum(
            jnp.max(jnp.maximum(jnp.maximum(batch[0], batch[1]), jnp.maximum(batch[2], batch[3])), axis=0, keepdims=True),
            jnp.max(jnp.maximum(jnp.maximum(hard[0], hard[1]), jnp.maximum(hard[2], hard[3])), axis=0, keepdims=True),
        )
        total = jnp.sum(sum(jnp.exp(b - top) for b in batch), axis=0, keepdims=True)
        total = total + jnp.sum(sum(jnp.exp(h - top) for h in hard), axis=0, keepdims=True)
        for to in range(NZ):
            sent[to, l : l + 1, :] = top
            sent[to, 2 + l : 3 + l, :] = total
    for to in range(NZ):
        sent[to, 4:8, :] = jnp.zeros((4, 128), F32)


def row_logs(stats, zp):
    logs = []
    for l in range(2):
        tops = jnp.where(zp == 0, stats[:, 0, l, :], stats[:, 1, l, :])
        totals = jnp.where(zp == 0, stats[:, 0, 2 + l, :], stats[:, 1, 2 + l, :])
        top = jnp.max(tops, axis=0, keepdims=True)
        logs.append(top + jnp.log(jnp.sum(totals * jnp.exp(tops - top), axis=0, keepdims=True)))
    return jnp.concatenate(logs, axis=1)


def block_weights(scores, o, logs, want, targets):
    h, a = o // 2, o % 2
    batch = jnp.concatenate([scores[h * 2 + l, a * 32 : (a + 1) * 32, :] for l in range(2)], axis=1)
    hard = jnp.concatenate([scores[h * 2 + l, 64 + a : 65 + a, :] for l in range(2)], axis=1)
    weights = jnp.exp(batch - logs)
    if targets and o == 0:
        row = lax.broadcasted_iota(jnp.int32, (32, ROWS), 0)
        lane = lax.broadcasted_iota(jnp.int32, (32, ROWS), 1)
        weights = weights - (lane == lax.axis_index("zh") * 32 + row).astype(F32)
    line = lax.broadcasted_iota(jnp.int32, (224, ROWS), 0)
    hard = jnp.where(line == want, jnp.exp(hard - logs), 0.0)
    return jnp.concatenate([weights.astype(BF16), hard.astype(BF16)], axis=0)


def share_kernel(stats, scores, asked, *refs):
    columns, (sent, logs, total) = refs[:4], refs[4:]
    zp = lax.axis_index("zp")
    near = row_logs(stats, zp)
    logs[0:1, :] = near
    logs[1:2, :] = row_logs(stats, 1 - zp)
    for o in range(NB):
        weights = block_weights(scores, o, near, asked[o : o + 1, :], True)
        cols = columns[o % 4][o // 4 * 256 : (o // 4 + 1) * 256, :]
        term = lax.dot_general(weights, cols, (((0,), (0,)), ((), ())), preferred_element_type=F32)
        if o == 0:
            total[...] = term
        elif o < NB - 1:
            total[...] += term
        else:
            sent[...] = (total[...] + term).astype(BF16).reshape(NH, 32, 512)


def column_grad_kernel(logs, scores, asked, queries, far_scores, far, keep, give, far_queries, far_asked):
    unpack(far, slice(4, 8), far_queries, far_asked)
    near_queries, other_queries = queries[...], far_queries[...]
    for o in range(4):
        weights = block_weights(scores, o, logs[0:1, :], asked[o : o + 1, :], True)
        grad = jnp.dot(weights, near_queries, preferred_element_type=F32)
        weights = block_weights(far_scores, o, logs[1:2, :], far_asked[o : o + 1, :], False)
        grad = grad + jnp.dot(weights, other_queries, preferred_element_type=F32)
        (give if o % 2 else keep)[o // 2] = grad.astype(BF16)


def pair_kernel(keep, came, own, sent):
    own[...] = keep[0].astype(F32) + came[0].astype(F32)
    sent[...] = (keep[1].astype(F32) + came[1].astype(F32)).astype(BF16)


def last_kernel(own, came, q_came, query_out, passage_out, negative_out):
    passage_out[...] = (own[0:32, :] + came[0:32, :].astype(F32)).astype(BF16)
    negative_out[...] = (own[32:256, :] + came[32:256, :].astype(F32)).astype(BF16)
    total = q_came[0].astype(F32)
    for z in range(1, NH):
        total = total + q_came[z].astype(F32)
    query_out[...] = total.astype(BF16)


def swap(x, axis):
    return lax.ppermute(x, axis, [(0, 1), (1, 0)])


def exchange(x, axes):
    return lax.all_to_all(x, axes, split_axis=0, concat_axis=0, tiled=True)


def shards(queries, passages, negatives, hard_owner, hard_row):
    sent, col0 = call(
        pack_kernel, [((NH, 144, 128), BF16), ((256, 512), BF16)],
        queries, hard_owner.T, hard_row.T, negatives, passages, hbm=5, limit=PACK_LIMIT,
        scratch=[
            pltpu.VMEM((32, 512), BF16), pltpu.VMEM((2, 7, 32), jnp.int32), pltpu.VMEM((2, 7, 128), jnp.int32),
            pltpu.SemaphoreType.DMA((5,)),
        ],
    )
    by_yh, by_zp = swap(col0, "yh"), swap(col0, "zp")
    near = exchange(sent, "zh")
    (pair,) = call(stack_kernel, [((512, 512), BF16)], col0, by_zp, cost=STACK_COST)
    (other,) = call(stack_kernel, [((512, 512), BF16)], by_yh, swap(by_zp, "yh"), cost=STACK_COST)
    columns = (pair, swap(pair, "c"), other, swap(other, "c"))
    parts, queries, asked = call(
        score_kernel, [((8, 72, 128), F32), ((ROWS, 512), BF16), ((NB, ROWS), jnp.int32)], near, *columns
    )
    far = swap(near, "zp")
    (summed,) = call(add_kernel, [((8, 72, 128), F32)], exchange(parts, ("yl", "x")), far)
    scores = exchange(summed, ("yl", "x"))
    stats, cross = call(stat_kernel, [((NZ, 8, 128), F32), ((4, 72, 128), F32)], scores)
    stats = exchange(stats, ("zh", "zp")).reshape(NH, 2, 8, 128)
    far_scores = swap(cross, "zp")
    q_part, logs = call(
        share_kernel, [((NH, 32, 512), BF16), ((8, ROWS), F32)], stats, scores, asked, *columns,
        scratch=[pltpu.VMEM((ROWS, 512), F32)],
    )
    q_came = exchange(q_part, "zh")
    keep, give = call(
        column_grad_kernel, [((2, 256, 512), BF16), ((2, 256, 512), BF16)],
        logs, scores, asked, queries, far_scores, far,
        scratch=[pltpu.VMEM((ROWS, 512), BF16), pltpu.VMEM((4, ROWS), jnp.int32)],
    )
    own, cross = call(pair_kernel, [((256, 512), F32), ((256, 512), BF16)], keep, swap(give, "c"))
    cross = swap(cross, "yh")
    return tuple(call(last_kernel, [((32, 512), BF16), ((32, 512), BF16), ((224, 512), BF16)], own, cross, q_came))


def solution(mesh):
    fine = Mesh(mesh.devices.reshape(2, NH, 2, 2, 2, 4), ("yh", "zh", "zp", "c", "yl", "x"))
    dp, mp = ("yh", "zh", "zp", "c"), ("yl", "x")
    return jax.shard_map(
        shards,
        mesh=fine,
        in_specs=(P(dp, mp), P(dp, mp), P(dp, mp), P(dp, None), P(dp, None)),
        out_specs=(P(dp, mp), P(dp, mp), P(dp, mp)),
        check_vma=False,
    )
```

```python
import math

import jax
import jax.numpy as jnp
from jax import lax
from jax.experimental import pallas as pl
from jax.experimental.pallas import tpu as pltpu
from jax.sharding import Mesh
from jax.sharding import PartitionSpec as P

BF16 = jnp.bfloat16
F32 = jnp.float32
NZ = 16
NH = 8
NB = 8
ROWS = 256
ABSENT = -1e30
VMEM_LIMIT = 48 * 1024 * 1024
PACK_LIMIT = 62 * 1024 * 1024
STACK_COST = pl.CostEstimate(flops=5765000000, bytes_accessed=0, transcendentals=0)


def call(kernel, out_shapes, *args, hbm=0, scratch=(), limit=VMEM_LIMIT, cost=None):
    specs = [pl.BlockSpec(memory_space=pl.ANY)] * hbm
    specs += [pl.BlockSpec(memory_space=pltpu.VMEM)] * (len(args) - hbm)
    return pl.pallas_call(
        kernel,
        out_shape=[jax.ShapeDtypeStruct(shape, dtype) for shape, dtype in out_shapes],
        in_specs=specs,
        out_specs=[pl.BlockSpec(memory_space=pltpu.VMEM)] * len(out_shapes),
        scratch_shapes=list(scratch),
        compiler_params=pltpu.CompilerParams(vmem_limit_bytes=limit),
        cost_estimate=cost,
    )(*args)


def pack_kernel(queries, owners, rows, negatives, passages, sent, columns, mine, short, wide, sems):
    copies = [
        pltpu.make_async_copy(owners, short.at[0], sems.at[0]),
        pltpu.make_async_copy(rows, short.at[1], sems.at[1]),
        pltpu.make_async_copy(queries, mine, sems.at[2]),
        pltpu.make_async_copy(negatives, columns.at[32:256], sems.at[3]),
        pltpu.make_async_copy(passages, columns.at[0:32], sems.at[4]),
    ]
    for copy in copies:
        copy.start()
    yh, zh, zp, c = (lax.axis_index(axis) for axis in ("yh", "zh", "zp", "c"))
    line = lax.broadcasted_iota(jnp.int32, (NH * 16, 128), 0)
    lane = lax.broadcasted_iota(jnp.int32, (NH * 16, 128), 1)
    block = line % 16
    z = (line // 16) * 2 + (zp ^ (block // 4))
    owner = ((yh ^ (block // 2 % 2)) * NZ + z) * 2 + (c ^ (block % 2))
    owner = jnp.where((block < NB) & (lane // 32 == zh % 4), owner, -2)
    copies[0].wait()
    copies[1].wait()
    for j in range(4):
        wide[:, :, j * 32 : (j + 1) * 32] = short[...]
    asked = jnp.full((NH * 16, 128), -1, jnp.int32)
    for k in range(short.shape[1]):
        asked = jnp.where(wide[0, k : k + 1, :] == owner, wide[1, k : k + 1, :], asked)
    asked = asked.astype(F32).astype(BF16)
    for to in range(NH):
        sent[to, 128:144, :] = asked[to * 16 : (to + 1) * 16, :]
    copies[2].wait()
    for to in range(NH):
        for l in range(4):
            sent[to, l * 32 : (l + 1) * 32, :] = mine[:, l * 128 : (l + 1) * 128]
    copies[3].wait()
    copies[4].wait()


def unpack(came, lines, queries, asked):
    for z in range(NH):
        for l in range(4):
            queries[z * 32 : (z + 1) * 32, l * 128 : (l + 1) * 128] = came[z, l * 32 : (l + 1) * 32, :]
    for g in range(2):
        rows = came[4 * g, 128:144, :].astype(F32)
        for z in range(4 * g + 1, 4 * g + 4):
            rows = jnp.maximum(rows, came[z, 128:144, :].astype(F32))
        asked[:, g * 128 : (g + 1) * 128] = rows[lines, :].astype(jnp.int32)


def stack_kernel(first, second, both):
    both[0:256, :] = first[...]
    both[256:512, :] = second[...]


def score_kernel(near, *refs):
    columns, (parts, queries, asked) = refs[:4], refs[4:]
    scale = 3.0 / math.sqrt(4096)
    unpack(near, slice(0, NB), queries, asked)
    every = queries[...]
    place = lax.broadcasted_iota(jnp.int32, (224, ROWS), 0)
    for o in range(NB):
        cols = columns[o % 4][o // 4 * 256 : (o // 4 + 1) * 256, :]
        part = lax.dot_general(cols, every, (((1,), (1,)), ((), ())), preferred_element_type=F32)
        want = asked[o : o + 1, :]
        hard = jnp.sum(jnp.where(place == want, part[32:256, :], 0.0), axis=0, keepdims=True) * scale
        hard = jnp.where(want >= 0, hard, ABSENT)
        h, a = o // 2, o % 2
        for l in range(2):
            lanes = slice(l * 128, (l + 1) * 128)
            parts[h * 2 + l, a * 32 : (a + 1) * 32, :] = part[0:32, lanes] * scale
            parts[h * 2 + l, 64 + a : 65 + a, :] = hard[:, lanes]
            if a == 1:
                parts[h * 2 + l, 66:72, :] = jnp.zeros((6, 128), F32)


def add_kernel(came, far, sent):
    total = came[0]
    for i in range(1, 8):
        total = total + came[i]
    for i in range(8):
        sent[i] = total


def stat_kernel(scores, sent, cross, tops):
    cross[...] = scores[4:8]
    for l in range(2):
        batch = [scores[h * 2 + l, 0:64, :] for h in range(4)]
        hard = [scores[h * 2 + l, 64:66, :] for h in range(4)]
        top = jnp.maximum(
            jnp.max(jnp.maximum(jnp.maximum(batch[0], batch[1]), jnp.maximum(batch[2], batch[3])), axis=0, keepdims=True),
            jnp.max(jnp.maximum(jnp.maximum(hard[0], hard[1]), jnp.maximum(hard[2], hard[3])), axis=0, keepdims=True),
        )
        total = jnp.sum(sum(jnp.exp(b - top) for b in batch), axis=0, keepdims=True)
        total = total + jnp.sum(sum(jnp.exp(h - top) for h in hard), axis=0, keepdims=True)
        tops[:, l * 128 : (l + 1) * 128] = top
        for to in range(NZ):
            sent[to, l : l + 1, :] = top
            sent[to, 2 + l : 3 + l, :] = total
    for to in range(NZ):
        sent[to, 4:8, :] = jnp.zeros((4, 128), F32)


def row_logs(stats, zp):
    logs = []
    for l in range(2):
        tops = jnp.where(zp == 0, stats[:, 0, l, :], stats[:, 1, l, :])
        totals = jnp.where(zp == 0, stats[:, 0, 2 + l, :], stats[:, 1, 2 + l, :])
        top = jnp.max(tops, axis=0, keepdims=True)
        logs.append(top + jnp.log(jnp.sum(totals * jnp.exp(tops - top), axis=0, keepdims=True)))
    return jnp.concatenate(logs, axis=1)


def is_target():
    row = lax.broadcasted_iota(jnp.int32, (32, ROWS), 0)
    lane = lax.broadcasted_iota(jnp.int32, (32, ROWS), 1)
    return lane == lax.axis_index("zh") * 32 + row


def batch_scores(scores, o):
    h, a = o // 2, o % 2
    return jnp.concatenate([scores[h * 2 + l, a * 32 : (a + 1) * 32, :] for l in range(2)], axis=1)


def block_weights(scores, o, logs, want, target):
    h, a = o // 2, o % 2
    hard = jnp.concatenate([scores[h * 2 + l, 64 + a : 65 + a, :] for l in range(2)], axis=1)
    weights = jnp.exp(batch_scores(scores, o) - logs)
    if target is not None and o == 0:
        weights = jnp.where(is_target(), target(weights), weights)
    line = lax.broadcasted_iota(jnp.int32, (224, ROWS), 0)
    hard = jnp.where(line == want, jnp.exp(hard - logs), 0.0)
    return jnp.concatenate([weights.astype(BF16), hard.astype(BF16)], axis=0)


def share_kernel(tops, scores, asked, *refs):
    columns, (total,) = refs[:4], refs[4:]
    for o in range(NB):
        weights = block_weights(scores, o, tops[...], asked[o : o + 1, :], jnp.zeros_like)
        cols = columns[o % 4][o // 4 * 256 : (o // 4 + 1) * 256, :]
        term = lax.dot_general(weights, cols, (((0,), (0,)), ((), ())), preferred_element_type=F32)
        if o == 0:
            total[...] = term
        else:
            total[...] += term


def scale_kernel(stats, tops, scores, total, own, sent, logs, turned):
    zh, zp = lax.axis_index("zh"), lax.axis_index("zp")
    near = row_logs(stats, zp)
    logs[0:1, :] = near
    logs[1:2, :] = row_logs(stats, 1 - zp)
    factors = jnp.exp(tops[...] - near)
    at_target = jnp.exp(batch_scores(scores, 0) - near) - 1.0
    at_target = jnp.sum(jnp.where(is_target(), at_target, 0.0), axis=0, keepdims=True)
    at_target = at_target.astype(BF16).astype(F32)
    for l in range(2):
        lanes = slice(l * 128, (l + 1) * 128)
        both = jnp.concatenate([factors[:, lanes], at_target[:, lanes], jnp.zeros((126, 128), F32)], axis=0)
        turned[lanes, :] = both.T
        part = total[lanes, :] * turned[lanes, 0:1]
        sent[l * 4 : (l + 1) * 4] = part.astype(BF16).reshape(4, 32, 512)
    mine = pl.ds(pl.multiple_of(zh * 32, 32), 32)
    part = total[mine, :] * turned[mine, 0:1] + own[0:32, :].astype(F32) * turned[mine, 1:2]
    sent[zh] = part.astype(BF16)


def column_grad_kernel(came, logs, scores, asked, queries, far, keep, give, far_queries, far_asked, far_scores, sem):
    copy = pltpu.make_async_copy(came, far_scores, sem)
    copy.start()
    unpack(far, slice(4, 8), far_queries, far_asked)
    near_queries, other_queries = queries[...], far_queries[...]
    for o in range(4):
        weights = block_weights(scores, o, logs[0:1, :], asked[o : o + 1, :], lambda w: w - 1.0)
        grad = jnp.dot(weights, near_queries, preferred_element_type=F32)
        if o == 0:
            copy.wait()
        weights = block_weights(far_scores, o, logs[1:2, :], far_asked[o : o + 1, :], None)
        grad = grad + jnp.dot(weights, other_queries, preferred_element_type=F32)
        (give if o % 2 else keep)[o // 2] = grad.astype(BF16)


def pair_kernel(keep, came, own, sent):
    own[...] = keep[0].astype(F32) + came[0].astype(F32)
    sent[...] = (keep[1].astype(F32) + came[1].astype(F32)).astype(BF16)


def last_kernel(own, came, q_came, query_out, passage_out, negative_out):
    passage_out[...] = (own[0:32, :] + came[0:32, :].astype(F32)).astype(BF16)
    negative_out[...] = (own[32:256, :] + came[32:256, :].astype(F32)).astype(BF16)
    total = q_came[0].astype(F32)
    for z in range(1, NH):
        total = total + q_came[z].astype(F32)
    query_out[...] = total.astype(BF16)


def swap(x, axis):
    return lax.ppermute(x, axis, [(0, 1), (1, 0)])


def exchange(x, axes):
    return lax.all_to_all(x, axes, split_axis=0, concat_axis=0, tiled=True)


def shards(queries, passages, negatives, hard_owner, hard_row):
    sent, col0 = call(
        pack_kernel, [((NH, 144, 128), BF16), ((256, 512), BF16)],
        queries, hard_owner.T, hard_row.T, negatives, passages, hbm=5, limit=PACK_LIMIT,
        scratch=[
            pltpu.VMEM((32, 512), BF16), pltpu.VMEM((2, 7, 32), jnp.int32), pltpu.VMEM((2, 7, 128), jnp.int32),
            pltpu.SemaphoreType.DMA((5,)),
        ],
    )
    by_yh, by_zp = swap(col0, "yh"), swap(col0, "zp")
    near = exchange(sent, "zh")
    (pair,) = call(stack_kernel, [((512, 512), BF16)], col0, by_zp, cost=STACK_COST)
    (other,) = call(stack_kernel, [((512, 512), BF16)], by_yh, swap(by_zp, "yh"), cost=STACK_COST)
    columns = (pair, swap(pair, "c"), other, swap(other, "c"))
    parts, queries, asked = call(
        score_kernel, [((8, 72, 128), F32), ((ROWS, 512), BF16), ((NB, ROWS), jnp.int32)], near, *columns
    )
    far = swap(near, "zp")
    (summed,) = call(add_kernel, [((8, 72, 128), F32)], exchange(parts, ("yl", "x")), far)
    scores = exchange(summed, ("yl", "x"))
    stats, cross, tops = call(
        stat_kernel, [((NZ, 8, 128), F32), ((4, 72, 128), F32), ((1, ROWS), F32)], scores
    )
    stats = exchange(stats, ("zh", "zp")).reshape(NH, 2, 8, 128)
    far_scores = swap(cross, "zp")
    (total,) = call(share_kernel, [((ROWS, 512), F32)], tops, scores, asked, *columns)
    q_part, logs = call(
        scale_kernel, [((NH, 32, 512), BF16), ((8, ROWS), F32)], stats, tops, scores, total, pair,
        scratch=[pltpu.VMEM((ROWS, 128), F32)],
    )
    q_came = exchange(q_part, "zh")
    keep, give = call(
        column_grad_kernel, [((2, 256, 512), BF16), ((2, 256, 512), BF16)],
        far_scores, logs, scores, asked, queries, far, hbm=1,
        scratch=[
            pltpu.VMEM((ROWS, 512), BF16), pltpu.VMEM((4, ROWS), jnp.int32), pltpu.VMEM((4, 72, 128), F32),
            pltpu.SemaphoreType.DMA,
        ],
    )
    own, cross = call(pair_kernel, [((256, 512), F32), ((256, 512), BF16)], keep, swap(give, "c"))
    cross = swap(cross, "yh")
    return tuple(call(last_kernel, [((32, 512), BF16), ((32, 512), BF16), ((224, 512), BF16)], own, cross, q_came))


def solution(mesh):
    fine = Mesh(mesh.devices.reshape(2, NH, 2, 2, 2, 4), ("yh", "zh", "zp", "c", "yl", "x"))
    dp, mp = ("yh", "zh", "zp", "c"), ("yl", "x")
    return jax.shard_map(
        shards,
        mesh=fine,
        in_specs=(P(dp, mp), P(dp, mp), P(dp, mp), P(dp, None), P(dp, None)),
        out_specs=(P(dp, mp), P(dp, mp), P(dp, mp)),
        check_vma=False,
    )
```

```python
import math

import jax
import jax.numpy as jnp
from jax import lax
from jax.experimental import pallas as pl
from jax.experimental.pallas import tpu as pltpu
from jax.sharding import Mesh
from jax.sharding import PartitionSpec as P

BF16 = jnp.bfloat16
F32 = jnp.float32
NZ = 16
NH = 8
NB = 8
ROWS = 256
ABSENT = -1e30
VMEM_LIMIT = 48 * 1024 * 1024
PACK_LIMIT = 62 * 1024 * 1024
STACK_COST = pl.CostEstimate(flops=5765000000, bytes_accessed=0, transcendentals=0)


def call(kernel, out_shapes, *args, hbm=0, scratch=(), limit=VMEM_LIMIT, cost=None):
    specs = [pl.BlockSpec(memory_space=pl.ANY)] * hbm
    specs += [pl.BlockSpec(memory_space=pltpu.VMEM)] * (len(args) - hbm)
    return pl.pallas_call(
        kernel,
        out_shape=[jax.ShapeDtypeStruct(shape, dtype) for shape, dtype in out_shapes],
        in_specs=specs,
        out_specs=[pl.BlockSpec(memory_space=pltpu.VMEM)] * len(out_shapes),
        scratch_shapes=list(scratch),
        compiler_params=pltpu.CompilerParams(vmem_limit_bytes=limit),
        cost_estimate=cost,
    )(*args)


def pack_kernel(queries, owners, rows, negatives, passages, sent, columns, mine, short, wide, sems):
    copies = [
        pltpu.make_async_copy(owners, short.at[0], sems.at[0]),
        pltpu.make_async_copy(rows, short.at[1], sems.at[1]),
        pltpu.make_async_copy(queries, mine, sems.at[2]),
        pltpu.make_async_copy(negatives, columns.at[32:256], sems.at[3]),
        pltpu.make_async_copy(passages, columns.at[0:32], sems.at[4]),
    ]
    for copy in copies:
        copy.start()
    yh, zh, zp, c = (lax.axis_index(axis) for axis in ("yh", "zh", "zp", "c"))
    line = lax.broadcasted_iota(jnp.int32, (NH * 16, 128), 0)
    lane = lax.broadcasted_iota(jnp.int32, (NH * 16, 128), 1)
    block = line % 16
    z = (line // 16) * 2 + (zp ^ (block // 4))
    owner = ((yh ^ (block // 2 % 2)) * NZ + z) * 2 + (c ^ (block % 2))
    owner = jnp.where((block < NB) & (lane // 32 == zh % 4), owner, -2)
    copies[0].wait()
    copies[1].wait()
    for j in range(4):
        wide[:, :, j * 32 : (j + 1) * 32] = short[...]
    asked = jnp.full((NH * 16, 128), -1, jnp.int32)
    for k in range(short.shape[1]):
        asked = jnp.where(wide[0, k : k + 1, :] == owner, wide[1, k : k + 1, :], asked)
    asked = asked.astype(F32).astype(BF16)
    for to in range(NH):
        sent[to, 128:144, :] = asked[to * 16 : (to + 1) * 16, :]
    copies[2].wait()
    for to in range(NH):
        for l in range(4):
            sent[to, l * 32 : (l + 1) * 32, :] = mine[:, l * 128 : (l + 1) * 128]
    copies[3].wait()
    copies[4].wait()


def unpack(came, lines, queries, asked):
    for z in range(NH):
        for l in range(4):
            queries[z * 32 : (z + 1) * 32, l * 128 : (l + 1) * 128] = came[z, l * 32 : (l + 1) * 32, :]
    for g in range(2):
        rows = came[4 * g, 128:144, :].astype(F32)
        for z in range(4 * g + 1, 4 * g + 4):
            rows = jnp.maximum(rows, came[z, 128:144, :].astype(F32))
        asked[:, g * 128 : (g + 1) * 128] = rows[lines, :].astype(jnp.int32)


def stack_kernel(first, second, both):
    both[0:256, :] = first[...]
    both[256:512, :] = second[...]


def score_kernel(near, *refs):
    columns, (parts, queries, asked) = refs[:4], refs[4:]
    scale = 3.0 / math.sqrt(4096)
    unpack(near, slice(0, NB), queries, asked)
    every = queries[...]
    place = lax.broadcasted_iota(jnp.int32, (224, ROWS), 0)
    for o in range(NB):
        cols = columns[o % 4][o // 4 * 256 : (o // 4 + 1) * 256, :]
        part = lax.dot_general(cols, every, (((1,), (1,)), ((), ())), preferred_element_type=F32)
        want = asked[o : o + 1, :]
        hard = jnp.sum(jnp.where(place == want, part[32:256, :], 0.0), axis=0, keepdims=True) * scale
        hard = jnp.where(want >= 0, hard, ABSENT)
        h, a = o // 2, o % 2
        for l in range(2):
            lanes = slice(l * 128, (l + 1) * 128)
            parts[h * 2 + l, a * 32 : (a + 1) * 32, :] = part[0:32, lanes] * scale
            parts[h * 2 + l, 64 + a : 65 + a, :] = hard[:, lanes]
            if a == 1:
                parts[h * 2 + l, 66:72, :] = jnp.zeros((6, 128), F32)


def add_kernel(came, far, sent):
    total = came[0]
    for i in range(1, 8):
        total = total + came[i]
    for i in range(8):
        sent[i] = total


def stat_kernel(scores, sent, cross, tops):
    cross[...] = scores[4:8]
    lines = {}
    for l in range(2):
        batch = [scores[h * 2 + l, 0:64, :] for h in range(4)]
        hard = [scores[h * 2 + l, 64:66, :] for h in range(4)]
        top = jnp.maximum(
            jnp.max(jnp.maximum(jnp.maximum(batch[0], batch[1]), jnp.maximum(batch[2], batch[3])), axis=0, keepdims=True),
            jnp.max(jnp.maximum(jnp.maximum(hard[0], hard[1]), jnp.maximum(hard[2], hard[3])), axis=0, keepdims=True),
        )
        total = jnp.sum(sum(jnp.exp(b - top) for b in batch), axis=0, keepdims=True)
        total = total + jnp.sum(sum(jnp.exp(h - top) for h in hard), axis=0, keepdims=True)
        tops[:, l * 128 : (l + 1) * 128] = top
        lines[l], lines[2 + l] = top, total
    tile = jnp.concatenate([lines[i] for i in range(4)] + [jnp.zeros((4, 128), F32)], axis=0)
    for to in range(NZ):
        sent[to] = tile


def row_logs(stats, zp):
    logs = []
    for l in range(2):
        tops = jnp.where(zp == 0, stats[:, 0, l, :], stats[:, 1, l, :])
        totals = jnp.where(zp == 0, stats[:, 0, 2 + l, :], stats[:, 1, 2 + l, :])
        top = jnp.max(tops, axis=0, keepdims=True)
        logs.append(top + jnp.log(jnp.sum(totals * jnp.exp(tops - top), axis=0, keepdims=True)))
    return jnp.concatenate(logs, axis=1)


def is_target():
    row = lax.broadcasted_iota(jnp.int32, (32, ROWS), 0)
    lane = lax.broadcasted_iota(jnp.int32, (32, ROWS), 1)
    return lane == lax.axis_index("zh") * 32 + row


def batch_scores(scores, o):
    h, a = o // 2, o % 2
    return jnp.concatenate([scores[h * 2 + l, a * 32 : (a + 1) * 32, :] for l in range(2)], axis=1)


def block_weights(scores, o, logs, want, target):
    h, a = o // 2, o % 2
    hard = jnp.concatenate([scores[h * 2 + l, 64 + a : 65 + a, :] for l in range(2)], axis=1)
    weights = jnp.exp(batch_scores(scores, o) - logs)
    if target is not None and o == 0:
        weights = jnp.where(is_target(), target(weights), weights)
    line = lax.broadcasted_iota(jnp.int32, (224, ROWS), 0)
    hard = jnp.where(line == want, jnp.exp(hard - logs), 0.0)
    return jnp.concatenate([weights.astype(BF16), hard.astype(BF16)], axis=0)


def share_kernel(tops, scores, asked, *refs):
    columns, (total,) = refs[:4], refs[4:]
    for o in range(NB):
        weights = block_weights(scores, o, tops[...], asked[o : o + 1, :], jnp.zeros_like)
        cols = columns[o % 4][o // 4 * 256 : (o // 4 + 1) * 256, :]
        term = lax.dot_general(weights, cols, (((0,), (0,)), ((), ())), preferred_element_type=F32)
        if o == 0:
            total[...] = term
        else:
            total[...] += term


def scale_kernel(stats, tops, scores, total, own, sent, logs, turned):
    zh, zp = lax.axis_index("zh"), lax.axis_index("zp")
    near = row_logs(stats, zp)
    logs[0:1, :] = near
    logs[1:2, :] = row_logs(stats, 1 - zp)
    factors = jnp.exp(tops[...] - near)
    at_target = jnp.exp(batch_scores(scores, 0) - near) - 1.0
    at_target = jnp.sum(jnp.where(is_target(), at_target, 0.0), axis=0, keepdims=True)
    at_target = at_target.astype(BF16).astype(F32)
    for l in range(2):
        lanes = slice(l * 128, (l + 1) * 128)
        both = jnp.concatenate([factors[:, lanes], at_target[:, lanes], jnp.zeros((126, 128), F32)], axis=0)
        turned[lanes, :] = both.T
        part = total[lanes, :] * turned[lanes, 0:1]
        sent[l * 4 : (l + 1) * 4] = part.astype(BF16).reshape(4, 32, 512)
    mine = pl.ds(pl.multiple_of(zh * 32, 32), 32)
    part = total[mine, :] * turned[mine, 0:1] + own[0:32, :].astype(F32) * turned[mine, 1:2]
    sent[zh] = part.astype(BF16)


def column_grad_kernel(came, logs, scores, asked, queries, far, keep, give, far_queries, far_asked, far_scores, sem):
    copy = pltpu.make_async_copy(came, far_scores, sem)
    copy.start()
    unpack(far, slice(4, 8), far_queries, far_asked)
    near_queries, other_queries = queries[...], far_queries[...]
    for o in range(4):
        weights = block_weights(scores, o, logs[0:1, :], asked[o : o + 1, :], lambda w: w - 1.0)
        grad = jnp.dot(weights, near_queries, preferred_element_type=F32)
        if o == 0:
            copy.wait()
        weights = block_weights(far_scores, o, logs[1:2, :], far_asked[o : o + 1, :], None)
        grad = grad + jnp.dot(weights, other_queries, preferred_element_type=F32)
        (give if o % 2 else keep)[o // 2] = grad.astype(BF16)


def pair_kernel(keep, came, own, sent):
    own[...] = keep[0].astype(F32) + came[0].astype(F32)
    sent[...] = (keep[1].astype(F32) + came[1].astype(F32)).astype(BF16)


def last_kernel(own, came, q_came, query_out, passage_out, negative_out):
    passage_out[...] = (own[0:32, :] + came[0:32, :].astype(F32)).astype(BF16)
    negative_out[...] = (own[32:256, :] + came[32:256, :].astype(F32)).astype(BF16)
    total = q_came[0].astype(F32)
    for z in range(1, NH):
        total = total + q_came[z].astype(F32)
    query_out[...] = total.astype(BF16)


def swap(x, axis):
    return lax.ppermute(x, axis, [(0, 1), (1, 0)])


def exchange(x, axes):
    return lax.all_to_all(x, axes, split_axis=0, concat_axis=0, tiled=True)


def shards(queries, passages, negatives, hard_owner, hard_row):
    sent, col0 = call(
        pack_kernel, [((NH, 144, 128), BF16), ((256, 512), BF16)],
        queries, hard_owner.T, hard_row.T, negatives, passages, hbm=5, limit=PACK_LIMIT,
        scratch=[
            pltpu.VMEM((32, 512), BF16), pltpu.VMEM((2, 7, 32), jnp.int32), pltpu.VMEM((2, 7, 128), jnp.int32),
            pltpu.SemaphoreType.DMA((5,)),
        ],
    )
    by_yh, by_zp = swap(col0, "yh"), swap(col0, "zp")
    near = exchange(sent, "zh")
    (pair,) = call(stack_kernel, [((512, 512), BF16)], col0, by_zp, cost=STACK_COST)
    (other,) = call(stack_kernel, [((512, 512), BF16)], by_yh, swap(by_zp, "yh"), cost=STACK_COST)
    columns = (pair, swap(pair, "c"), other, swap(other, "c"))
    parts, queries, asked = call(
        score_kernel, [((8, 72, 128), F32), ((ROWS, 512), BF16), ((NB, ROWS), jnp.int32)], near, *columns
    )
    far = swap(near, "zp")
    (summed,) = call(add_kernel, [((8, 72, 128), F32)], exchange(parts, ("yl", "x")), far)
    scores = exchange(summed, ("yl", "x"))
    stats, cross, tops = call(
        stat_kernel, [((NZ, 8, 128), F32), ((4, 72, 128), F32), ((1, ROWS), F32)], scores
    )
    stats = exchange(stats, ("zh", "zp")).reshape(NH, 2, 8, 128)
    far_scores = swap(cross, "zp")
    (total,) = call(share_kernel, [((ROWS, 512), F32)], tops, scores, asked, *columns)
    q_part, logs = call(
        scale_kernel, [((NH, 32, 512), BF16), ((8, ROWS), F32)], stats, tops, scores, total, pair,
        scratch=[pltpu.VMEM((ROWS, 128), F32)],
    )
    q_came = exchange(q_part, "zh")
    keep, give = call(
        column_grad_kernel, [((2, 256, 512), BF16), ((2, 256, 512), BF16)],
        far_scores, logs, scores, asked, queries, far, hbm=1,
        scratch=[
            pltpu.VMEM((ROWS, 512), BF16), pltpu.VMEM((4, ROWS), jnp.int32), pltpu.VMEM((4, 72, 128), F32),
            pltpu.SemaphoreType.DMA,
        ],
    )
    own, cross = call(pair_kernel, [((256, 512), F32), ((256, 512), BF16)], keep, swap(give, "c"))
    cross = swap(cross, "yh")
    return tuple(call(last_kernel, [((32, 512), BF16), ((32, 512), BF16), ((224, 512), BF16)], own, cross, q_came))


def solution(mesh):
    fine = Mesh(mesh.devices.reshape(2, NH, 2, 2, 2, 4), ("yh", "zh", "zp", "c", "yl", "x"))
    dp, mp = ("yh", "zh", "zp", "c"), ("yl", "x")
    return jax.shard_map(
        shards,
        mesh=fine,
        in_specs=(P(dp, mp), P(dp, mp), P(dp, mp), P(dp, None), P(dp, None)),
        out_specs=(P(dp, mp), P(dp, mp), P(dp, mp)),
        check_vma=False,
    )
```
